256 devices in a mesh: src: 8 (over z_lo, core), brick: 32 (over x, y, z_hi).
Axes of the slice: x: 4, y: 4, z: 8 (z_hi: 2, z_lo: 4; z = z_hi * 4 + z_lo), core: 2. Of those that a mesh axis runs over, the one named last changes fastest.
Arguments:
- slowness: float32 [128, 64, 128], P('brick'), may hold values from 0.5 to 2
- source_x: int32 [16], P('src'), may hold values from 0 to 127
- source_y: int32 [16], P('src'), may hold values from 0 to 63
- source_z: int32 [16], P('src'), may hold values from 0 to 127
- station_x: int32 [2048], replicated, may hold values from 0 to 127
- station_y: int32 [2048], replicated, may hold values from 0 to 63
- station_z: int32 [2048], replicated, may hold values from 0 to 127
- observed: float32 [16, 2048], P('src'), may hold values from 0 to 4
Outputs:
- kernel: float32 [128, 64, 128], P('brick', 'src')
- arrivals: float32 [16, 2048], P('src', 'brick')
The draws below stay inside these ranges and needn't reach their ends.
All inputs are finite; a program needn't handle non-finite values.
Results may differ from the reference program's by a relative error of at most 0.0003.
Values sent between devices are 32-bit elements; how exact they have to be, the bound alone decides.
No kernel may reach another device: no remote copies, remote signals or barrier semaphores. Data moves between devices by JAX's collectives and lax.ppermute only.
A program may use at most 128 MiB of HBM per device.

```python
import math
import jax
import jax.numpy as jnp
from jax import lax

NY = 64
NZ = 128
REC = 2048
ITERS = 16
NX = 128
SOURCES = 16


def touch_ends(values, key, low, high):
    extent = values.shape
    spot = [jax.random.randint(jax.random.fold_in(key, axis), (), 0, extent[axis]) for axis in range(len(extent))]
    values = values.at[tuple(spot)].set(low)
    longest = extent.index(max(extent))
    spot[longest] = (spot[longest] + 1) % extent[longest]
    return values.at[tuple(spot)].set(high)


def steps_of(key, extent, shards, low, largest):
    def one(position, parts):
        draws = jax.random.uniform(jax.random.fold_in(jax.random.fold_in(key, 6), position), (parts,), jnp.float32, low / len(shards), largest / len(shards))
        return jnp.repeat(jnp.exp(draws), extent[position] // parts).reshape((-1,) + (1,) * (len(extent) - position - 1))

    loudness = one(*shards[0])
    for cut in shards[1:]:
        loudness = loudness * one(*cut)
    return loudness


def setup_inputs(seed: int = 0) -> dict:
    key_list = jax.random.split(jax.random.key(seed), 9)
    return {
        "slowness": jnp.clip(jnp.exp(math.log(2.0) - 1.3862944 * jax.random.uniform(key_list[0], (NX, NY, NZ), jnp.float32) ** steps_of(key_list[0], (NX, NY, NZ), ((0, 32),), -0.2, 0.2)), 0.5, 2.0),
        "source_x": touch_ends(jax.random.randint(key_list[1], (SOURCES,), 0, NX), jax.random.fold_in(key_list[1], 1), 0, NX - 1).astype(jnp.int32),
        "source_y": touch_ends(jax.random.randint(key_list[2], (SOURCES,), 0, NY), jax.random.fold_in(key_list[2], 1), 0, NY - 1).astype(jnp.int32),
        "source_z": touch_ends(jax.random.randint(key_list[3], (SOURCES,), 0, NZ), jax.random.fold_in(key_list[3], 1), 0, NZ - 1).astype(jnp.int32),
        "station_x": touch_ends(jax.random.randint(key_list[4], (REC,), 0, NX), jax.random.fold_in(key_list[4], 1), 0, NX - 1).astype(jnp.int32),
        "station_y": touch_ends(jax.random.randint(key_list[5], (REC,), 0, NY), jax.random.fold_in(key_list[5], 1), 0, NY - 1).astype(jnp.int32),
        "station_z": touch_ends(jax.random.randint(key_list[6], (REC,), 0, NZ), jax.random.fold_in(key_list[6], 1), 0, NZ - 1).astype(jnp.int32),
        "observed": jnp.clip(4.0 * jax.random.uniform(key_list[7], (SOURCES, REC), jnp.float32) ** steps_of(key_list[7], (SOURCES, REC), ((0, 8),), -0.2, 0.2), 0.0, 4.0),
    }


spacing = 0.015625
big_value = 1000000.0
start_slowness = 2.0

def neighbours(padded):
    return [padded[2:, 1:-1, 1:-1], padded[:-2, 1:-1, 1:-1], padded[1:-1, 2:, 1:-1], padded[1:-1, :-2, 1:-1], padded[1:-1, 1:-1, 2:], padded[1:-1, 1:-1, :-2]]

def reference(slowness, source_x, source_y, source_z, station_x, station_y, station_z, observed):
    slow_pad = jnp.pad(slowness, 1, constant_values=1.0)
    costs = [spacing * 0.5 * (slowness + other) for other in neighbours(slow_pad)]
    grid_x = jnp.arange(NX, dtype=jnp.float32)[:, None, None]
    grid_y = jnp.arange(NY, dtype=jnp.float32)[None, :, None]
    grid_z = jnp.arange(NZ, dtype=jnp.float32)[None, None, :]
    flat = ((station_x * NY + station_y) * NZ + station_z).astype(jnp.int32)

    def forward_sweep(step, times):
        padded = jnp.pad(times, 1, constant_values=big_value)
        fresh = times
        for cost, other in zip(costs, neighbours(padded)):
            fresh = jnp.minimum(fresh, other + cost)
        return fresh

    def one_source(total, inputs):
        sx, sy, sz, seen = inputs
        dist = (grid_x - sx.astype(jnp.float32)) ** 2 + (grid_y - sy.astype(jnp.float32)) ** 2 + (grid_z - sz.astype(jnp.float32)) ** 2
        times = start_slowness * spacing * jnp.sqrt(dist)
        times = lax.fori_loop(0, ITERS, forward_sweep, times)
        arrive = times.reshape(-1)[flat]
        source = jnp.zeros((NX * NY * NZ,), jnp.float32).at[flat].add(arrive - seen).reshape(NX, NY, NZ)
        low_pad = jnp.pad(times, 1, constant_values=-big_value)
        weights = [jnp.maximum(other - times, 0.0) / spacing for other in neighbours(low_pad)]
        denom = 1.0 + weights[0] + weights[1] + weights[2] + weights[3] + weights[4] + weights[5]

        def adjoint_sweep(step, field):
            padded = jnp.pad(field, 1)
            acc = source
            for weight, other in zip(weights, neighbours(padded)):
                acc = acc + weight * other
            return acc / denom
        field = lax.fori_loop(0, ITERS, adjoint_sweep, jnp.zeros((NX, NY, NZ), jnp.float32))
        return (total + field, arrive)
    summed, arrivals = lax.scan(one_source, jnp.zeros((NX, NY, NZ), jnp.float32), (source_x, source_y, source_z, observed))
    return (slowness * summed, arrivals)
```

```python
import jax
import jax.numpy as jnp
from jax import lax
from jax.experimental import pallas as pl
from jax.experimental.pallas import tpu as pltpu
from jax.sharding import Mesh, PartitionSpec as P

ITERS = 16
SPACING = 0.015625
BIG = 1000000.0
START = 2.0

LAYERS = 8
SEEN = 48
WIDE = SEEN + 2 * ITERS
ADJ = LAYERS + 2 * ITERS
NX, NY, NZ = 128, 64, 128


def iota(shape, dim):
    return lax.broadcasted_iota(jnp.int32, shape, dim)


def station_kernel(meta, sx, sy, sz, obs, count_out, seen_out, rhs):
    half, base = meta[0], meta[1]
    row = (sx[...] - base) * 64 + (sy[...] % 8) * 8 + sy[...] // 8
    seen = jnp.where(half == 0, obs[0:1, :], obs[1:2, :])
    hi = seen.astype(jnp.bfloat16).astype(jnp.float32)
    mid = (seen - hi).astype(jnp.bfloat16).astype(jnp.float32)
    low = seen - hi - mid
    there = iota((NZ, sx.shape[1]), 0) == sz[...]
    for part, value in enumerate((jnp.ones_like(seen), hi, mid, low)):
        rhs[part * NZ : (part + 1) * NZ, :] = jnp.where(there, value, 0.0).astype(jnp.bfloat16)
    chunk = 256

    def body(step, carry):
        match = iota((chunk, sx.shape[1]), 0) + step * chunk == row
        match = jnp.where(match, 1.0, 0.0).astype(jnp.bfloat16)
        got = lax.dot_general(
            match, rhs[...], (((1,), (1,)), ((), ())), preferred_element_type=jnp.float32
        )
        where = pl.ds(pl.multiple_of(step * chunk, chunk), chunk)
        count_out[where, :] = got[:, :NZ]
        seen_out[where, :] = got[:, NZ : 2 * NZ] + got[:, 2 * NZ : 3 * NZ] + got[:, 3 * NZ :]
        return carry

    lax.fori_loop(0, ADJ * 64 // chunk, body, 0)


def forward_kernel(meta, src_x, src_y, src_z, rows, lanes, mine, other, times_out, arrive_out, slow, even, odd, picked):
    half, core, offset, first = meta[0], meta[2], meta[3], meta[4]
    pos_x = src_x[half]
    pos_y = src_y[half]
    pos_z = src_z[half]
    row_y = iota((8, 8, NZ), 1) * 8 + iota((8, 8, NZ), 0) - pos_y
    row_z = iota((8, 8, NZ), 2) - pos_z
    dist_yz = (row_y * row_y + row_z * row_z).astype(jnp.float32)

    def load(layer, carry):
        a, b = mine[offset + layer], other[offset + layer]
        cells = jnp.concatenate([jnp.where(core == 0, a, b), jnp.where(core == 0, b, a)], axis=0)
        x = first + layer
        inside = (x >= 0) & (x < NX)
        dx = (x - pos_x).astype(jnp.float32)
        start = START * SPACING * jnp.sqrt(dist_yz + dx * dx)
        slow[layer] = jnp.where(inside, SPACING * cells, BIG)
        even[layer] = jnp.where(inside, start + (0.5 * SPACING) * cells, BIG)
        return carry

    lax.fori_loop(0, WIDE, load, 0, unroll=2)
    lane = iota((8, NZ), 1)
    sub = iota((8, NZ), 0)
    step = 2

    def sweep(before, after, k):
        def body(j, carry):
            layer = k + j * step
            near = before[pl.ds(layer - 1, step + 2)]
            here = near[1 : step + 1]
            best = jnp.minimum(near[:step], near[2:])
            left = jnp.where(lane == 0, BIG, pltpu.roll(here, 1, 3))
            right = jnp.where(lane == NZ - 1, BIG, pltpu.roll(here, NZ - 1, 3))
            best = jnp.minimum(best, jnp.minimum(left, right))
            down = jnp.where(sub == 0, BIG, pltpu.roll(here[:, 7:8], 1, 2))
            up = jnp.where(sub == 7, BIG, pltpu.roll(here[:, 0:1], 7, 2))
            below = jnp.concatenate([down, here[:, :7]], axis=1)
            above = jnp.concatenate([here[:, 1:], up], axis=1)
            best = jnp.minimum(best, jnp.minimum(below, above))
            after[pl.ds(layer, step)] = jnp.minimum(here, best + slow[pl.ds(layer, step)])
            return carry

        lax.fori_loop(0, (WIDE - 2 * k) // step, body, 0)

    for k in range(1, ITERS + 1):
        sweep(*((even, odd) if k % 2 else (odd, even)), k)

    def finish(layer, carry):
        x = first + ITERS + layer
        cells = even[ITERS + layer] - 0.5 * slow[ITERS + layer]
        cells = jnp.where((x >= 0) & (x < NX), cells, -BIG)
        times_out[pl.ds(pl.multiple_of(layer * 64, 64), 64), :] = cells.reshape(64, NZ)
        return carry

    lax.fori_loop(0, SEEN, finish, 0, unroll=2)
    one = iota((1, NZ), 1)

    def pick(j, carry):
        line = times_out[pl.ds(rows[j], 1), :]
        picked[pl.ds(j, 1), :] = jnp.where(one == lanes[j], line, 0.0)
        return carry

    lax.fori_loop(0, picked.shape[0], pick, 0, unroll=16)
    arrive_out[...] = lax.dot_general(
        jnp.ones((8, NZ), jnp.float32),
        picked[...],
        (((1,), (1,)), ((), ())),
        precision=lax.Precision.HIGHEST,
        preferred_element_type=jnp.float32,
    )


def adjoint_kernel(meta, times, count, seen, out, coef, even, odd):
    start = meta[5]
    lane = iota((8, NZ), 1)
    sub = iota((8, NZ), 0)

    def weights(layer, carry):
        here = times[start + layer]
        left = jnp.where(lane == 0, -BIG, pltpu.roll(here, 1, 2))
        right = jnp.where(lane == NZ - 1, -BIG, pltpu.roll(here, NZ - 1, 2))
        down = jnp.where(sub == 0, -BIG, pltpu.roll(here[7:8], 1, 1))
        up = jnp.where(sub == 7, -BIG, pltpu.roll(here[0:1], 7, 1))
        below = jnp.concatenate([down, here[:7]], axis=0)
        above = jnp.concatenate([here[1:], up], axis=0)
        others = (times[start + layer + 1], times[start + layer - 1], above, below, right, left)
        terms = [jnp.maximum(n - here, 0.0) * (1.0 / SPACING) for n in others]
        denom = 1.0 + terms[0] + terms[1] + terms[2] + terms[3] + terms[4] + terms[5]
        scale = 1.0 / denom
        for n, term in enumerate(terms):
            coef[n, layer] = term * scale
        first = (count[layer] * here - seen[layer]) * scale
        coef[6, layer] = first
        even[layer] = first
        return carry

    lax.fori_loop(1, ADJ - 1, weights, 0)
    step = 2

    def sweep(before, after, k):
        def body(j, carry):
            layer = k + j * step
            where = pl.ds(layer, step)
            near = before[pl.ds(layer - 1, step + 2)]
            here = near[1 : step + 1]
            left = pltpu.roll(here, 1, 3)
            right = pltpu.roll(here, NZ - 1, 3)
            below = jnp.concatenate([pltpu.roll(here[:, 7:8], 1, 2), here[:, :7]], axis=1)
            above = jnp.concatenate([here[:, 1:], pltpu.roll(here[:, 0:1], 7, 2)], axis=1)
            total = coef[6, where] + coef[0, where] * near[2:] + coef[1, where] * near[:step]
            total = total + coef[2, where] * above + coef[3, where] * below
            after[where] = total + (coef[4, where] * right + coef[5, where] * left)
            return carry

        lax.fori_loop(0, (ADJ - 2 * k) // step, body, 0)

    for k in range(2, ITERS + 1):
        sweep(*((odd, even) if k % 2 else (even, odd)), k)
    final = odd if ITERS % 2 == 0 else even
    for layer in range(LAYERS):
        for i in range(8):
            out[pl.ds(layer * 8 + i, 8, stride=64), :] = final[ITERS + layer, i]


def cycle(cells, axis, size, shift):
    return lax.ppermute(cells, axis, [(i, (i + shift) % size) for i in range(size)])


def gathered(cells, core, y, half):
    cells = cells.reshape(4, 8, 2, 4, NZ).transpose(0, 2, 3, 1, 4)
    part = lax.dynamic_index_in_dim(cells, core, 1, keepdims=False)
    partner = cycle(part, "half", 2, 1)
    slab = jnp.where(
        half == 0, jnp.concatenate([part, partner]), jnp.concatenate([partner, part])
    )
    line = jnp.zeros((4,) + slab.shape, jnp.float32)
    line = lax.dynamic_update_index_in_dim(line, slab, y, 0)
    for shift in (1, 3, 2):
        line = lax.dynamic_update_index_in_dim(line, cycle(slab, "y", 4, shift), (y - shift) % 4, 0)
    block = line.reshape((32,) + slab.shape[1:])
    before = lax.ppermute(block, "x", [(0, 1), (1, 2), (2, 3)])
    after = lax.ppermute(block, "x", [(1, 0), (2, 1), (3, 2)])
    mine = jnp.concatenate([before, block, after])
    return mine, cycle(mine, "core", 2, 1)


VMEM = pl.BlockSpec(memory_space=pltpu.VMEM)
SMEM = pl.BlockSpec(memory_space=pltpu.SMEM)


def f32(*shape):
    return jax.ShapeDtypeStruct(shape, jnp.float32)


def per_device(slowness, source_x, source_y, source_z, station_x, station_y, station_z, observed):
    core, x, y, half = (lax.axis_index(a) for a in ("core", "x", "y", "half"))
    group = lax.axis_index("zlo") * 2 + core
    slab = 4 * x + y
    back = jnp.where(y < 2, 16, 24)
    seen_first = slab * LAYERS - back
    slow_first = seen_first - ITERS
    meta = jnp.stack(
        [half, slab * LAYERS - ITERS, core, slow_first - 32 * (x - 1), slow_first, back - ITERS]
    ).astype(jnp.int32)

    stations = station_x.shape[0]
    params = pltpu.CompilerParams(vmem_limit_bytes=28 * 1024 * 1024)
    count, seen = pl.pallas_call(
        station_kernel,
        out_shape=(f32(ADJ * 64, NZ), f32(ADJ * 64, NZ)),
        in_specs=[SMEM, VMEM, VMEM, VMEM, VMEM],
        out_specs=(VMEM, VMEM),
        scratch_shapes=[pltpu.VMEM((4 * NZ, stations), jnp.bfloat16)],
        compiler_params=params,
        cost_estimate=pl.CostEstimate(
            flops=2 * ADJ * 64 * stations * 4 * NZ, bytes_accessed=2 * ADJ * 64 * NZ * 4, transcendentals=0
        ),
        name="stations",
    )(meta, station_x.reshape(1, -1), station_y.reshape(1, -1), station_z.reshape(1, -1), observed)

    def line_of(values):
        return lax.dynamic_index_in_dim(values.reshape(4, 4, stations // 16), y, 1, keepdims=False)

    at_x, at_y, at_z = line_of(station_x), line_of(station_y), line_of(station_z)
    owned = at_x // 32 == x
    rows = jnp.where(owned, (at_x - seen_first) * 64 + (at_y % 8) * 8 + at_y // 8, 0).reshape(-1)
    lanes = jnp.where(owned, at_z, -1).reshape(-1)

    mine, other = gathered(slowness, core, y, half)
    times, arrive = pl.pallas_call(
        forward_kernel,
        out_shape=(f32(SEEN * 64, NZ), f32(8, stations // 4)),
        in_specs=[SMEM] * 6 + [VMEM, VMEM],
        out_specs=(VMEM, VMEM),
        scratch_shapes=[
            pltpu.VMEM((WIDE, 8, 8, NZ), jnp.float32),
            pltpu.VMEM((WIDE, 8, 8, NZ), jnp.float32),
            pltpu.VMEM((WIDE, 8, 8, NZ), jnp.float32),
            pltpu.VMEM((stations // 4, NZ), jnp.float32),
        ],
        compiler_params=params,
        cost_estimate=pl.CostEstimate(
            flops=7 * ITERS * WIDE * 8192, bytes_accessed=WIDE * 8192 * 8, transcendentals=WIDE * 8192
        ),
        name="forward",
    )(meta, source_x, source_y, source_z, rows, lanes, mine, other)

    arrive = arrive[0].reshape(4, stations // 16)
    got = lax.dynamic_index_in_dim(arrive, x, 0)
    for shift in (1, 2, 3):
        piece = lax.dynamic_index_in_dim(arrive, (x + shift) % 4, 0)
        got = got + cycle(piece, "x", 4, shift)

    pieces = pl.pallas_call(
        adjoint_kernel,
        out_shape=f32(512, NZ),
        in_specs=[SMEM, VMEM, VMEM, VMEM],
        out_specs=VMEM,
        scratch_shapes=[
            pltpu.VMEM((7, ADJ, 8, 8, NZ), jnp.float32),
            pltpu.VMEM((ADJ, 8, 8, NZ), jnp.float32),
            pltpu.VMEM((ADJ, 8, 8, NZ), jnp.float32),
        ],
        compiler_params=params,
        cost_estimate=pl.CostEstimate(
            flops=12 * ITERS * ADJ * 8192, bytes_accessed=4 * ADJ * 8192 * 4, transcendentals=ADJ * 8192
        ),
        name="adjoint",
    )(
        meta,
        times.reshape(SEEN, 8, 8, NZ),
        count.reshape(ADJ, 8, 8, NZ),
        seen.reshape(ADJ, 8, 8, NZ),
    )
    summed = jnp.sum(
        lax.all_to_all(pieces.reshape(16, 4, 8, NZ), ("zlo", "core", "half"), 0, 0, tiled=True), axis=0
    )
    kernel = lax.dynamic_slice(slowness, (0, group * 8, 0), (4, 8, NZ)) * summed

    got = got.reshape(2, stations // 32)
    own = lax.dynamic_index_in_dim(got, half, 0)
    partner = cycle(lax.dynamic_index_in_dim(got, 1 - half, 0), "half", 2, 1)
    arrivals = jnp.where(half == 0, jnp.concatenate([own, partner]), jnp.concatenate([partner, own]))
    return kernel, arrivals


def solution(mesh):
    fine = Mesh(mesh.devices.reshape(4, 2, 4, 4, 2), ("zlo", "core", "x", "y", "half"))
    src, brick = ("zlo", "core"), ("x", "y", "half")
    in_specs = (P(brick, None, None), P(src), P(src), P(src), P(), P(), P(), P(src, None))
    out_specs = (P(brick, src, None), P(src, brick))
    return jax.shard_map(
        per_device, mesh=fine, in_specs=in_specs, out_specs=out_specs, check_vma=False
    )
```

```python
import jax
import jax.numpy as jnp
from jax import lax
from jax.experimental import pallas as pl
from jax.experimental.pallas import tpu as pltpu
from jax.sharding import Mesh, PartitionSpec as P

ITERS = 16
SPACING = 0.015625
BIG = 1000000.0
START = 2.0

LAYERS = 8
SEEN = 48
WIDE = SEEN + 2 * ITERS
ADJ = LAYERS + 2 * ITERS
NX, NY, NZ = 128, 64, 128
HALF = NZ // 2


def iota(shape, dim):
    return lax.broadcasted_iota(jnp.int32, shape, dim)


def parts(values):
    hi = values.astype(jnp.bfloat16).astype(jnp.float32)
    mid = (values - hi).astype(jnp.bfloat16).astype(jnp.float32)
    return hi, mid, values - hi - mid


def moved(values, inverse):
    z, lane = iota((NZ, NZ), 0), iota((NZ, NZ), 1)
    if inverse:
        z, lane = lane, z
    match = jnp.where((z % 2) * HALF + z // 2 == lane, 1.0, 0.0).astype(jnp.bfloat16)
    got = [
        jnp.dot(part.astype(jnp.bfloat16), match, preferred_element_type=jnp.float32)
        for part in parts(values)
    ]
    return got[0] + got[1] + got[2]


def paired(first, second, low):
    axis = first.ndim - 1
    even = jnp.where(low, first, pltpu.roll(second, HALF, axis))
    odd = jnp.where(low, pltpu.roll(first, HALF, axis), second)
    return jnp.stack([even, odd])


def parted(even, odd, low):
    axis = even.ndim - 1
    first = jnp.where(low, even, pltpu.roll(odd, HALF, axis))
    second = jnp.where(low, pltpu.roll(even, HALF, axis), odd)
    return first, second


def beside(here, edge):
    lane = iota((8, NZ), 1) % HALF
    sub = iota((8, NZ), 0)

    def bounded(mask, values):
        return values if edge is None else jnp.where(mask, edge, values)

    even, odd = here[:, 0:1], here[:, 1:2]
    same = jnp.concatenate([odd, even], axis=1)
    left = bounded(lane == 0, pltpu.roll(odd, 1, 4))
    right = bounded(lane == HALF - 1, pltpu.roll(even, NZ - 1, 4))
    rolled = jnp.concatenate([left, right], axis=1)
    down = bounded(sub == 0, pltpu.roll(here[:, :, 7:8], 1, 3))
    up = bounded(sub == 7, pltpu.roll(here[:, :, 0:1], 7, 3))
    below = jnp.concatenate([down, here[:, :, :7]], axis=2)
    above = jnp.concatenate([here[:, :, 1:], up], axis=2)
    return same, rolled, below, above


def sweeps(first, last, count, step, even, odd, block):
    for k in range(first, last + 1):
        before, after = (even, odd) if k % 2 == first % 2 else (odd, even)
        whole, rest = divmod(count - k, step)

        def body(j, carry, before=before, after=after, k=k):
            block(before, after, k + j * step, step)
            return carry

        lax.fori_loop(0, whole, body, 0)
        if rest:
            block(before, after, count - rest, rest)
        after[count] = pltpu.roll(after[count - 1], HALF, 3)
    return after


def prepare_kernel(meta, cells, out):
    core = meta[2]
    rows = [
        cells[pl.ds(layer * NY + 4 * core + i, 8, stride=8), :] for layer in range(4) for i in range(4)
    ]
    out[...] = moved(jnp.concatenate(rows), False)


def station_kernel(meta, sx, sy, sz, obs, count_out, seen_out, rhs):
    half, base = meta[0], meta[1]
    x, y, z = sx[...] - base, sy[...], sz[...]
    layer = jnp.minimum(x, ADJ - 1 - x)
    row = (layer * 2 + z % 2) * NY + (y % 8) * 8 + y // 8
    row = jnp.where(layer >= 0, row, -1)
    lane = jnp.where(x < ADJ // 2, 0, HALF) + z // 2
    seen = jnp.where(half == 0, obs[0:1, :], obs[1:2, :])
    there = iota((NZ, sx.shape[1]), 0) == lane
    for part, value in enumerate((jnp.ones_like(seen),) + parts(seen)):
        rhs[part * NZ : (part + 1) * NZ, :] = jnp.where(there, value, 0.0).astype(jnp.bfloat16)
    chunk = 256

    def body(step, carry):
        match = iota((chunk, sx.shape[1]), 0) + step * chunk == row
        match = jnp.where(match, 1.0, 0.0).astype(jnp.bfloat16)
        got = lax.dot_general(
            match, rhs[...], (((1,), (1,)), ((), ())), preferred_element_type=jnp.float32
        )
        where = pl.ds(pl.multiple_of(step * chunk, chunk), chunk)
        count_out[where, :] = got[:, :NZ]
        seen_out[where, :] = got[:, NZ : 2 * NZ] + got[:, 2 * NZ : 3 * NZ] + got[:, 3 * NZ :]
        return carry

    lax.fori_loop(0, ADJ * NY // chunk, body, 0)


def forward_kernel(meta, src_x, src_y, src_z, rows, lanes, mine, other, times_out, arrive_out, slow, even, odd, table, picked):
    half, core, offset, first = meta[0], meta[2], meta[3], meta[4]
    shape = (2, 8, 8, NZ)
    low = iota((8, NZ), 1) < HALF
    dy = iota(shape, 2) * 8 + iota(shape, 1) - src_y[half]
    dz = iota(shape, 3) % HALF * 2 + iota(shape, 0) - src_z[half]
    dist_yz = (dy * dy + dz * dz).astype(jnp.float32)
    row_x = jnp.where(low, first, first + WIDE - 1)
    sign = jnp.where(low, 1, -1)

    def of_layer(layer):
        a, b = mine[offset + layer], other[offset + layer]
        return jnp.concatenate([jnp.where(core == 0, a, b), jnp.where(core == 0, b, a)], axis=0)

    def load(layer, carry):
        cells = paired(of_layer(layer), of_layer(WIDE - 1 - layer), low)
        x = row_x + sign * layer
        inside = (x >= 0) & (x < NX)
        dx = (x - src_x[half]).astype(jnp.float32)
        start = START * SPACING * jnp.sqrt(dist_yz + dx * dx)
        slow[layer] = jnp.where(inside, SPACING * cells, BIG)
        even[layer] = jnp.where(inside, start + (0.5 * SPACING) * cells, BIG)
        return carry

    lax.fori_loop(0, WIDE // 2, load, 0, unroll=4)

    def block(before, after, layer, step):
        near = before[pl.ds(layer - 1, step + 2)]
        here = near[1 : step + 1]
        best = jnp.minimum(near[:step], near[2:])
        same, rolled, below, above = beside(here, BIG)
        best = jnp.minimum(best, jnp.minimum(same, rolled))
        best = jnp.minimum(best, jnp.minimum(below, above))
        after[pl.ds(layer, step)] = jnp.minimum(here, best + slow[pl.ds(layer, step)])

    even[WIDE // 2] = pltpu.roll(even[WIDE // 2 - 1], HALF, 3)
    last = sweeps(1, ITERS, WIDE // 2, 16, even, odd, block)

    def finish(j, carry):
        layer = ITERS + j
        x = row_x + sign * layer
        cells = last[layer] - 0.5 * slow[layer]
        cells = jnp.where((x >= 0) & (x < NX), cells, -BIG)
        table[pl.ds(pl.multiple_of(j * 2 * NY, 2 * NY), 2 * NY), :] = cells.reshape(2 * NY, NZ)
        times_out[j], times_out[SEEN - 1 - j] = parted(cells[0], cells[1], low)
        return carry

    lax.fori_loop(0, SEEN // 2, finish, 0, unroll=4)
    one = iota((1, NZ), 1)

    def pick(j, carry):
        line = table[pl.ds(rows[j], 1), :]
        picked[pl.ds(j, 1), :] = jnp.where(one == lanes[j], line, 0.0)
        return carry

    lax.fori_loop(0, picked.shape[0], pick, 0, unroll=16)
    arrive_out[...] = lax.dot_general(
        jnp.ones((8, NZ), jnp.float32),
        picked[...],
        (((1,), (1,)), ((), ())),
        precision=lax.Precision.HIGHEST,
        preferred_element_type=jnp.float32,
    )


def adjoint_kernel(meta, times, count, seen, out, coef, even, odd, natural):
    start = meta[5]
    low = iota((8, NZ), 1) < HALF
    top = ADJ // 2

    def load(layer, carry):
        odd[layer] = paired(times[start + layer], times[start + ADJ - 1 - layer], low)
        return carry

    lax.fori_loop(0, top, load, 0, unroll=4)
    odd[top] = pltpu.roll(odd[top - 1], HALF, 3)

    def weights(layer, carry):
        here = odd[pl.ds(layer, 1)]
        others = (odd[pl.ds(layer + 1, 1)], odd[pl.ds(layer - 1, 1)]) + beside(here, -BIG)
        terms = [jnp.maximum(n - here, 0.0) * (1.0 / SPACING) for n in others]
        denom = 1.0 + terms[0] + terms[1] + terms[2] + terms[3] + terms[4] + terms[5]
        scale = 1.0 / denom
        for n, term in enumerate(terms):
            coef[n, pl.ds(layer, 1)] = term * scale
        first = (count[pl.ds(layer, 1)] * here - seen[pl.ds(layer, 1)]) * scale
        coef[6, pl.ds(layer, 1)] = first
        even[pl.ds(layer, 1)] = first
        return carry

    lax.fori_loop(1, top, weights, 0)
    even[top] = pltpu.roll(even[top - 1], HALF, 3)

    def block(before, after, layer, step):
        where = pl.ds(layer, step)
        near = before[pl.ds(layer - 1, step + 2)]
        same, rolled, below, above = beside(near[1 : step + 1], None)
        total = coef[6, where] + coef[0, where] * near[2:] + coef[1, where] * near[:step]
        total = total + coef[2, where] * same + coef[4, where] * below
        after[where] = total + (coef[3, where] * rolled + coef[5, where] * above)

    final = sweeps(2, ITERS, top, 8, even, odd, block)
    for j in range(LAYERS // 2):
        cells = final[ITERS + j]
        natural[j], natural[LAYERS - 1 - j] = parted(cells[0], cells[1], low)
    rows = moved(natural[...].reshape(LAYERS * NY, NZ), True)
    for layer in range(LAYERS):
        for i in range(8):
            at = (layer * 8 + i) * 8
            out[pl.ds(layer * 8 + i, 8, stride=64), :] = rows[at : at + 8]


def cycle(cells, axis, size, shift):
    return lax.ppermute(cells, axis, [(i, (i + shift) % size) for i in range(size)])


def gathered(part, y, half, beside_it):
    partner = cycle(part, "half", 2, 1)
    slab = jnp.where(
        half == 0, jnp.concatenate([part, partner]), jnp.concatenate([partner, part])
    )
    line = jnp.zeros((4,) + slab.shape, jnp.float32)
    line = lax.dynamic_update_index_in_dim(line, slab, y, 0)
    for shift in (1, 3, 2):
        line = lax.dynamic_update_index_in_dim(line, cycle(slab, "y", 4, shift), (y - shift) % 4, 0)
    block = line.reshape((32,) + slab.shape[1:])
    before = lax.ppermute(block, "x", [(0, 1), (1, 2), (2, 3)])
    after = lax.ppermute(block, "x", [(1, 0), (2, 1), (3, 2)])
    before, after, beside_it = lax.optimization_barrier((before, after, beside_it))
    mine = jnp.concatenate([before, block, after])
    return mine, cycle(mine, "core", 2, 1), beside_it


VMEM = pl.BlockSpec(memory_space=pltpu.VMEM)
SMEM = pl.BlockSpec(memory_space=pltpu.SMEM)


def f32(*shape):
    return jax.ShapeDtypeStruct(shape, jnp.float32)


def per_device(slowness, source_x, source_y, source_z, station_x, station_y, station_z, observed):
    core, x, y, half = (lax.axis_index(a) for a in ("core", "x", "y", "half"))
    group = lax.axis_index("zlo") * 2 + core
    slab = 4 * x + y
    back = jnp.where(y < 2, 16, 24)
    seen_first = slab * LAYERS - back
    slow_first = seen_first - ITERS
    meta = jnp.stack(
        [half, slab * LAYERS - ITERS, core, slow_first - 32 * (x - 1), slow_first, back - ITERS]
    ).astype(jnp.int32)

    stations = station_x.shape[0]
    params = pltpu.CompilerParams(vmem_limit_bytes=28 * 1024 * 1024)
    count, seen = pl.pallas_call(
        station_kernel,
        out_shape=(f32(ADJ * 64, NZ), f32(ADJ * 64, NZ)),
        in_specs=[SMEM, VMEM, VMEM, VMEM, VMEM],
        out_specs=(VMEM, VMEM),
        scratch_shapes=[pltpu.VMEM((4 * NZ, stations), jnp.bfloat16)],
        compiler_params=params,
        cost_estimate=pl.CostEstimate(
            flops=2 * ADJ * 64 * stations * 4 * NZ, bytes_accessed=2 * ADJ * 64 * NZ * 4, transcendentals=0
        ),
        name="stations",
    )(meta, station_x.reshape(1, -1), station_y.reshape(1, -1), station_z.reshape(1, -1), observed)

    def line_of(values):
        return lax.dynamic_index_in_dim(values.reshape(4, 4, stations // 16), y, 1, keepdims=False)

    at_x, at_y, at_z = line_of(station_x), line_of(station_y), line_of(station_z)
    owned = at_x // 32 == x
    seen_x = at_x - seen_first
    layer = jnp.minimum(seen_x, SEEN - 1 - seen_x)
    row = (layer * 2 + at_z % 2) * NY + (at_y % 8) * 8 + at_y // 8
    rows = jnp.where(owned, row, 0).reshape(-1)
    lanes = jnp.where(owned, jnp.where(seen_x < SEEN // 2, 0, HALF) + at_z // 2, -1).reshape(-1)

    part = pl.pallas_call(
        prepare_kernel,
        out_shape=f32(128, NZ),
        in_specs=[SMEM, VMEM],
        out_specs=VMEM,
        compiler_params=params,
        name="prepare",
    )(meta, slowness.reshape(-1, NZ))
    mine, other, (count, seen) = gathered(part.reshape(4, 4, 8, NZ), y, half, (count, seen))
    times, arrive = pl.pallas_call(
        forward_kernel,
        out_shape=(f32(SEEN, 8, 8, NZ), f32(8, stations // 4)),
        in_specs=[SMEM] * 6 + [VMEM, VMEM],
        out_specs=(VMEM, VMEM),
        scratch_shapes=[
            pltpu.VMEM((WIDE // 2, 2, 8, 8, NZ), jnp.float32),
            pltpu.VMEM((WIDE // 2 + 1, 2, 8, 8, NZ), jnp.float32),
            pltpu.VMEM((WIDE // 2 + 1, 2, 8, 8, NZ), jnp.float32),
            pltpu.VMEM((SEEN * NY, NZ), jnp.float32),
            pltpu.VMEM((stations // 4, NZ), jnp.float32),
        ],
        compiler_params=params,
        cost_estimate=pl.CostEstimate(
            flops=7 * ITERS * WIDE * 8192, bytes_accessed=WIDE * 8192 * 8, transcendentals=WIDE * 8192
        ),
        name="forward",
    )(meta, source_x, source_y, source_z, rows, lanes, mine, other)

    arrive = arrive[0].reshape(4, stations // 16)
    got = lax.dynamic_index_in_dim(arrive, x, 0)
    for shift in (1, 2, 3):
        piece = lax.dynamic_index_in_dim(arrive, (x + shift) % 4, 0)
        got = got + cycle(piece, "x", 4, shift)

    pieces = pl.pallas_call(
        adjoint_kernel,
        out_shape=f32(512, NZ),
        in_specs=[SMEM, VMEM, VMEM, VMEM],
        out_specs=VMEM,
        scratch_shapes=[
            pltpu.VMEM((7, ADJ // 2, 2, 8, 8, NZ), jnp.float32),
            pltpu.VMEM((ADJ // 2 + 1, 2, 8, 8, NZ), jnp.float32),
            pltpu.VMEM((ADJ // 2 + 1, 2, 8, 8, NZ), jnp.float32),
            pltpu.VMEM((LAYERS, 8, 8, NZ), jnp.float32),
        ],
        compiler_params=params,
        cost_estimate=pl.CostEstimate(
            flops=12 * ITERS * ADJ * 8192, bytes_accessed=4 * ADJ * 8192 * 4, transcendentals=ADJ * 8192
        ),
        name="adjoint",
    )(
        meta,
        times,
        count.reshape(ADJ // 2, 2, 8, 8, NZ),
        seen.reshape(ADJ // 2, 2, 8, 8, NZ),
    )
    summed = jnp.sum(
        lax.all_to_all(pieces.reshape(16, 4, 8, NZ), ("zlo", "core", "half"), 0, 0, tiled=True), axis=0
    )
    kernel = lax.dynamic_slice(slowness, (0, group * 8, 0), (4, 8, NZ)) * summed

    got = got.reshape(2, stations // 32)
    own = lax.dynamic_index_in_dim(got, half, 0)
    partner = cycle(lax.dynamic_index_in_dim(got, 1 - half, 0), "half", 2, 1)
    arrivals = jnp.where(half == 0, jnp.concatenate([own, partner]), jnp.concatenate([partner, own]))
    return kernel, arrivals


def solution(mesh):
    fine = Mesh(mesh.devices.reshape(4, 2, 4, 4, 2), ("zlo", "core", "x", "y", "half"))
    src, brick = ("zlo", "core"), ("x", "y", "half")
    in_specs = (P(brick, None, None), P(src), P(src), P(src), P(), P(), P(), P(src, None))
    out_specs = (P(brick, src, None), P(src, brick))
    return jax.shard_map(
        per_device, mesh=fine, in_specs=in_specs, out_specs=out_specs, check_vma=False
    )
```

```python
import jax
import jax.numpy as jnp
from jax import lax
from jax.experimental import pallas as pl
from jax.experimental.pallas import tpu as pltpu
from jax.sharding import Mesh, PartitionSpec as P

ITERS = 16
SPACING = 0.015625
BIG = 1000000.0
START = 2.0

LAYERS = 8
SEEN = 48
WIDE = SEEN + 2 * ITERS
ADJ = LAYERS + 2 * ITERS
NX, NY, NZ = 128, 64, 128
HALF = NZ // 2


def iota(shape, dim):
    return lax.broadcasted_iota(jnp.int32, shape, dim)


def parts(values):
    hi = values.astype(jnp.bfloat16).astype(jnp.float32)
    mid = (values - hi).astype(jnp.bfloat16).astype(jnp.float32)
    return hi, mid, values - hi - mid


def moved(values, inverse):
    z, lane = iota((NZ, NZ), 0), iota((NZ, NZ), 1)
    if inverse:
        z, lane = lane, z
    match = jnp.where((z % 2) * HALF + z // 2 == lane, 1.0, 0.0).astype(jnp.bfloat16)
    got = [
        jnp.dot(part.astype(jnp.bfloat16), match, preferred_element_type=jnp.float32)
        for part in parts(values)
    ]
    return got[0] + got[1] + got[2]


def paired(first, second, low):
    axis = first.ndim - 1
    even = jnp.where(low, first, pltpu.roll(second, HALF, axis))
    odd = jnp.where(low, pltpu.roll(first, HALF, axis), second)
    return jnp.stack([even, odd])


def parted(even, odd, low):
    axis = even.ndim - 1
    first = jnp.where(low, even, pltpu.roll(odd, HALF, axis))
    second = jnp.where(low, pltpu.roll(even, HALF, axis), odd)
    return first, second


def lane_of(values, index):
    tiles = values.reshape(-1, 8, NZ)
    tiles = [
        jnp.take_along_axis(tiles[n], index, axis=1, mode="promise_in_bounds") for n in range(tiles.shape[0])
    ]
    return jnp.stack(tiles).reshape(values.shape)


def beside(here, edge, repeat=False):
    whole = iota((8, NZ), 1)
    lane = whole % HALF
    sub = iota((8, NZ), 0)

    def bounded(mask, values):
        return values if edge is None else jnp.where(mask, edge, values)

    even, odd = here[:, 0:1], here[:, 1:2]
    same = jnp.concatenate([odd, even], axis=1)
    if repeat:
        left = lane_of(odd, jnp.where(lane == 0, whole, whole - 1))
        right = lane_of(even, jnp.where(lane == HALF - 1, whole, whole + 1))
    else:
        left = bounded(lane == 0, pltpu.roll(odd, 1, 4))
        right = bounded(lane == HALF - 1, pltpu.roll(even, NZ - 1, 4))
    rolled = jnp.concatenate([left, right], axis=1)
    down = bounded(sub == 0, pltpu.roll(here[:, :, 7:8], 1, 3))
    up = bounded(sub == 7, pltpu.roll(here[:, :, 0:1], 7, 3))
    below = jnp.concatenate([down, here[:, :, :7]], axis=2)
    above = jnp.concatenate([here[:, :, 1:], up], axis=2)
    return same, rolled, below, above


def sweeps(first, last, count, step, even, odd, block):
    for k in range(first, last + 1):
        before, after = (even, odd) if k % 2 == first % 2 else (odd, even)
        whole, rest = divmod(count - k, step)

        def body(j, carry, before=before, after=after, k=k):
            block(before, after, k + j * step, step)
            return carry

        lax.fori_loop(0, whole, body, 0)
        if rest:
            block(before, after, count - rest, rest)
        after[count] = pltpu.roll(after[count - 1], HALF, 3)
    return after


def prepare_kernel(meta, cells, out):
    core = meta[2]
    rows = [
        cells[pl.ds(layer * NY + 4 * core + i, 8, stride=8), :] for layer in range(4) for i in range(4)
    ]
    out[...] = moved(jnp.concatenate(rows), False)


def station_kernel(meta, sx, sy, sz, obs, count_out, seen_out, rhs):
    half, base = meta[0], meta[1]
    x, y, z = sx[...] - base, sy[...], sz[...]
    layer = jnp.minimum(x, ADJ - 1 - x)
    row = (layer * 2 + z % 2) * NY + (y % 8) * 8 + y // 8
    row = jnp.where(layer >= 0, row, -1)
    lane = jnp.where(x < ADJ // 2, 0, HALF) + z // 2
    seen = jnp.where(half == 0, obs[0:1, :], obs[1:2, :])
    there = iota((NZ, sx.shape[1]), 0) == lane
    for part, value in enumerate((jnp.ones_like(seen),) + parts(seen)):
        rhs[part * NZ : (part + 1) * NZ, :] = jnp.where(there, value, 0.0).astype(jnp.bfloat16)
    chunk = 256

    def body(step, carry):
        match = iota((chunk, sx.shape[1]), 0) + step * chunk == row
        match = jnp.where(match, 1.0, 0.0).astype(jnp.bfloat16)
        got = lax.dot_general(
            match, rhs[...], (((1,), (1,)), ((), ())), preferred_element_type=jnp.float32
        )
        where = pl.ds(pl.multiple_of(step * chunk, chunk), chunk)
        count_out[where, :] = got[:, :NZ]
        seen_out[where, :] = got[:, NZ : 2 * NZ] + got[:, 2 * NZ : 3 * NZ] + got[:, 3 * NZ :]
        return carry

    lax.fori_loop(0, ADJ * NY // chunk, body, 0)


def forward_kernel(meta, src_x, src_y, src_z, rows, lanes, mine, other, times_out, arrive_out, slow, even, odd, table, picked):
    half, core, offset, first = meta[0], meta[2], meta[3], meta[4]
    shape = (2, 8, 8, NZ)
    low = iota((8, NZ), 1) < HALF
    dy = iota(shape, 2) * 8 + iota(shape, 1) - src_y[half]
    dz = iota(shape, 3) % HALF * 2 + iota(shape, 0) - src_z[half]
    dist_yz = (dy * dy + dz * dz).astype(jnp.float32)
    row_x = jnp.where(low, first, first + WIDE - 1)
    sign = jnp.where(low, 1, -1)

    def of_layer(layer):
        a, b = mine[offset + layer], other[offset + layer]
        return jnp.concatenate([jnp.where(core == 0, a, b), jnp.where(core == 0, b, a)], axis=0)

    def load(layer, carry):
        cells = paired(of_layer(layer), of_layer(WIDE - 1 - layer), low)
        x = row_x + sign * layer
        inside = (x >= 0) & (x < NX)
        dx = (x - src_x[half]).astype(jnp.float32)
        start = START * SPACING * jnp.sqrt(dist_yz + dx * dx)
        slow[layer] = jnp.where(inside, SPACING * cells, BIG)
        even[layer] = jnp.where(inside, start + (0.5 * SPACING) * cells, BIG)
        return carry

    lax.fori_loop(0, WIDE // 2, load, 0, unroll=4)

    def block(before, after, layer, step):
        near = before[pl.ds(layer - 1, step + 2)]
        here = near[1 : step + 1]
        best = jnp.minimum(near[:step], near[2:])
        same, rolled, below, above = beside(here, BIG, True)
        best = jnp.minimum(best, jnp.minimum(same, rolled))
        best = jnp.minimum(best, jnp.minimum(below, above))
        after[pl.ds(layer, step)] = jnp.minimum(here, best + slow[pl.ds(layer, step)])

    even[WIDE // 2] = pltpu.roll(even[WIDE // 2 - 1], HALF, 3)
    last = sweeps(1, ITERS, WIDE // 2, 20, even, odd, block)

    def finish(j, carry):
        layer = ITERS + j
        x = row_x + sign * layer
        cells = last[layer] - 0.5 * slow[layer]
        cells = jnp.where((x >= 0) & (x < NX), cells, -BIG)
        table[pl.ds(pl.multiple_of(j * 2 * NY, 2 * NY), 2 * NY), :] = cells.reshape(2 * NY, NZ)
        times_out[j], times_out[SEEN - 1 - j] = parted(cells[0], cells[1], low)
        return carry

    lax.fori_loop(0, SEEN // 2, finish, 0, unroll=4)
    one = iota((1, NZ), 1)

    def pick(j, carry):
        line = table[pl.ds(rows[j], 1), :]
        picked[pl.ds(j, 1), :] = jnp.where(one == lanes[j], line, 0.0)
        return carry

    lax.fori_loop(0, picked.shape[0], pick, 0, unroll=16)
    arrive_out[...] = lax.dot_general(
        jnp.ones((8, NZ), jnp.float32),
        picked[...],
        (((1,), (1,)), ((), ())),
        precision=lax.Precision.HIGHEST,
        preferred_element_type=jnp.float32,
    )


def adjoint_kernel(meta, times, count, seen, out, coef, even, odd, natural):
    start = meta[5]
    low = iota((8, NZ), 1) < HALF
    top = ADJ // 2

    def load(layer, carry):
        odd[layer] = paired(times[start + layer], times[start + ADJ - 1 - layer], low)
        return carry

    lax.fori_loop(0, top, load, 0, unroll=4)
    odd[top] = pltpu.roll(odd[top - 1], HALF, 3)

    def weights(layer, size):
        where = pl.ds(layer, size)
        here = odd[where]
        others = (odd[pl.ds(layer + 1, size)], odd[pl.ds(layer - 1, size)]) + beside(here, -BIG)
        terms = [jnp.maximum(n - here, 0.0) * (1.0 / SPACING) for n in others]
        denom = 1.0 + terms[0] + terms[1] + terms[2] + terms[3] + terms[4] + terms[5]
        scale = 1.0 / denom
        for n, term in enumerate(terms):
            coef[n, where] = term * scale
        first = (count[where] * here - seen[where]) * scale
        coef[6, where] = first
        even[where] = first

    lax.fori_loop(0, (top - 1) // 4, lambda j, carry: (weights(1 + 4 * j, 4), carry)[1], 0)
    weights(top - 3, 3)
    even[top] = pltpu.roll(even[top - 1], HALF, 3)

    def block(before, after, layer, step):
        where = pl.ds(layer, step)
        near = before[pl.ds(layer - 1, step + 2)]
        same, rolled, below, above = beside(near[1 : step + 1], None)
        total = coef[6, where] + coef[0, where] * near[2:] + coef[1, where] * near[:step]
        total = total + coef[2, where] * same + coef[4, where] * below
        after[where] = total + (coef[3, where] * rolled + coef[5, where] * above)

    final = sweeps(2, ITERS, top, 8, even, odd, block)
    for j in range(LAYERS // 2):
        cells = final[ITERS + j]
        natural[j], natural[LAYERS - 1 - j] = parted(cells[0], cells[1], low)
    rows = moved(natural[...].reshape(LAYERS * NY, NZ), True)
    for layer in range(LAYERS):
        for i in range(8):
            at = (layer * 8 + i) * 8
            out[pl.ds(layer * 8 + i, 8, stride=64), :] = rows[at : at + 8]


def cycle(cells, axis, size, shift):
    return lax.ppermute(cells, axis, [(i, (i + shift) % size) for i in range(size)])


def gathered(part, y, half, beside_it):
    partner = cycle(part, "half", 2, 1)
    slab = jnp.where(
        half == 0, jnp.concatenate([part, partner]), jnp.concatenate([partner, part])
    )
    line = jnp.zeros((4,) + slab.shape, jnp.float32)
    line = lax.dynamic_update_index_in_dim(line, slab, y, 0)
    for shift in (1, 3, 2):
        line = lax.dynamic_update_index_in_dim(line, cycle(slab, "y", 4, shift), (y - shift) % 4, 0)
    block = line.reshape((32,) + slab.shape[1:])
    before = lax.ppermute(block, "x", [(0, 1), (1, 2), (2, 3)])
    after = lax.ppermute(block, "x", [(1, 0), (2, 1), (3, 2)])
    before, after, beside_it = lax.optimization_barrier((before, after, beside_it))
    mine = jnp.concatenate([before, block, after])
    return mine, cycle(mine, "core", 2, 1), beside_it


VMEM = pl.BlockSpec(memory_space=pltpu.VMEM)
SMEM = pl.BlockSpec(memory_space=pltpu.SMEM)


def f32(*shape):
    return jax.ShapeDtypeStruct(shape, jnp.float32)


def per_device(slowness, source_x, source_y, source_z, station_x, station_y, station_z, observed):
    core, x, y, half = (lax.axis_index(a) for a in ("core", "x", "y", "half"))
    group = lax.axis_index("zlo") * 2 + core
    slab = 4 * x + y
    back = jnp.where(y < 2, 16, 24)
    seen_first = slab * LAYERS - back
    slow_first = seen_first - ITERS
    meta = jnp.stack(
        [half, slab * LAYERS - ITERS, core, slow_first - 32 * (x - 1), slow_first, back - ITERS]
    ).astype(jnp.int32)

    stations = station_x.shape[0]
    params = pltpu.CompilerParams(vmem_limit_bytes=28 * 1024 * 1024)
    count, seen = pl.pallas_call(
        station_kernel,
        out_shape=(f32(ADJ * 64, NZ), f32(ADJ * 64, NZ)),
        in_specs=[SMEM, VMEM, VMEM, VMEM, VMEM],
        out_specs=(VMEM, VMEM),
        scratch_shapes=[pltpu.VMEM((4 * NZ, stations), jnp.bfloat16)],
        compiler_params=params,
        cost_estimate=pl.CostEstimate(
            flops=2 * ADJ * 64 * stations * 4 * NZ, bytes_accessed=2 * ADJ * 64 * NZ * 4, transcendentals=0
        ),
        name="stations",
    )(meta, station_x.reshape(1, -1), station_y.reshape(1, -1), station_z.reshape(1, -1), observed)

    def line_of(values):
        return lax.dynamic_index_in_dim(values.reshape(4, 4, stations // 16), y, 1, keepdims=False)

    at_x, at_y, at_z = line_of(station_x), line_of(station_y), line_of(station_z)
    owned = at_x // 32 == x
    seen_x = at_x - seen_first
    layer = jnp.minimum(seen_x, SEEN - 1 - seen_x)
    row = (layer * 2 + at_z % 2) * NY + (at_y % 8) * 8 + at_y // 8
    rows = jnp.where(owned, row, 0).reshape(-1)
    lanes = jnp.where(owned, jnp.where(seen_x < SEEN // 2, 0, HALF) + at_z // 2, -1).reshape(-1)

    part = pl.pallas_call(
        prepare_kernel,
        out_shape=f32(128, NZ),
        in_specs=[SMEM, VMEM],
        out_specs=VMEM,
        compiler_params=params,
        name="prepare",
    )(meta, slowness.reshape(-1, NZ))
    mine, other, (count, seen) = gathered(part.reshape(4, 4, 8, NZ), y, half, (count, seen))
    times, arrive = pl.pallas_call(
        forward_kernel,
        out_shape=(f32(SEEN, 8, 8, NZ), f32(8, stations // 4)),
        in_specs=[SMEM] * 6 + [VMEM, VMEM],
        out_specs=(VMEM, VMEM),
        scratch_shapes=[
            pltpu.VMEM((WIDE // 2, 2, 8, 8, NZ), jnp.float32),
            pltpu.VMEM((WIDE // 2 + 1, 2, 8, 8, NZ), jnp.float32),
            pltpu.VMEM((WIDE // 2 + 1, 2, 8, 8, NZ), jnp.float32),
            pltpu.VMEM((SEEN * NY, NZ), jnp.float32),
            pltpu.VMEM((stations // 4, NZ), jnp.float32),
        ],
        compiler_params=params,
        cost_estimate=pl.CostEstimate(
            flops=7 * ITERS * WIDE * 8192, bytes_accessed=WIDE * 8192 * 8, transcendentals=WIDE * 8192
        ),
        name="forward",
    )(meta, source_x, source_y, source_z, rows, lanes, mine, other)

    arrive = arrive[0].reshape(4, 2, stations // 32)
    own = lax.dynamic_index_in_dim(arrive, half, 1, keepdims=False)
    partner = cycle(lax.dynamic_index_in_dim(arrive, 1 - half, 1, keepdims=False), "half", 2, 1)

    pieces = pl.pallas_call(
        adjoint_kernel,
        out_shape=f32(512, NZ),
        in_specs=[SMEM, VMEM, VMEM, VMEM],
        out_specs=VMEM,
        scratch_shapes=[
            pltpu.VMEM((7, ADJ // 2, 2, 8, 8, NZ), jnp.float32),
            pltpu.VMEM((ADJ // 2 + 1, 2, 8, 8, NZ), jnp.float32),
            pltpu.VMEM((ADJ // 2 + 1, 2, 8, 8, NZ), jnp.float32),
            pltpu.VMEM((LAYERS, 8, 8, NZ), jnp.float32),
        ],
        compiler_params=params,
        cost_estimate=pl.CostEstimate(
            flops=12 * ITERS * ADJ * 8192, bytes_accessed=4 * ADJ * 8192 * 4, transcendentals=ADJ * 8192
        ),
        name="adjoint",
    )(
        meta,
        times,
        count.reshape(ADJ // 2, 2, 8, 8, NZ),
        seen.reshape(ADJ // 2, 2, 8, 8, NZ),
    )
    pieces, own, partner = lax.optimization_barrier((pieces, own, partner))
    summed = jnp.sum(
        lax.all_to_all(pieces.reshape(16, 4, 8, NZ), ("zlo", "core", "half"), 0, 0, tiled=True), axis=0
    )
    kernel = lax.dynamic_slice(slowness, (0, group * 8, 0), (4, 8, NZ)) * summed

    known = jnp.where(half == 0, jnp.stack([own, partner], 1), jnp.stack([partner, own], 1))
    arrivals = lax.dynamic_index_in_dim(known, x, 0, keepdims=False)
    for shift in (1, 2, 3):
        piece = lax.dynamic_index_in_dim(known, (x + shift) % 4, 0, keepdims=False)
        arrivals = arrivals + cycle(piece, "x", 4, shift)
    return kernel, arrivals


def solution(mesh):
    fine = Mesh(mesh.devices.reshape(4, 2, 4, 4, 2), ("zlo", "core", "x", "y", "half"))
    src, brick = ("zlo", "core"), ("x", "y", "half")
    in_specs = (P(brick, None, None), P(src), P(src), P(src), P(), P(), P(), P(src, None))
    out_specs = (P(brick, src, None), P(src, brick))
    return jax.shard_map(
        per_device, mesh=fine, in_specs=in_specs, out_specs=out_specs, check_vma=False
    )
```

```python
import jax
import jax.numpy as jnp
from jax import lax
from jax.experimental import pallas as pl
from jax.experimental.pallas import tpu as pltpu
from jax.sharding import Mesh, PartitionSpec as P

ITERS = 16
SPACING = 0.015625
BIG = 1000000.0
START = 2.0

LAYERS = 8
SEEN = 48
WIDE = SEEN + 2 * ITERS
ADJ = LAYERS + 2 * ITERS
NX, NY, NZ = 128, 64, 128
HALF = NZ // 2


def iota(shape, dim):
    return lax.broadcasted_iota(jnp.int32, shape, dim)


def parts(values):
    hi = values.astype(jnp.bfloat16).astype(jnp.float32)
    mid = (values - hi).astype(jnp.bfloat16).astype(jnp.float32)
    return hi, mid, values - hi - mid


def moved(values, inverse):
    z, lane = iota((NZ, NZ), 0), iota((NZ, NZ), 1)
    if inverse:
        z, lane = lane, z
    match = jnp.where((z % 2) * HALF + z // 2 == lane, 1.0, 0.0).astype(jnp.bfloat16)
    got = [
        jnp.dot(part.astype(jnp.bfloat16), match, preferred_element_type=jnp.float32)
        for part in parts(values)
    ]
    return got[0] + got[1] + got[2]


def paired(first, second, low):
    axis = first.ndim - 1
    even = jnp.where(low, first, pltpu.roll(second, HALF, axis))
    odd = jnp.where(low, pltpu.roll(first, HALF, axis), second)
    return jnp.stack([even, odd])


def parted(even, odd, low):
    axis = even.ndim - 1
    first = jnp.where(low, even, pltpu.roll(odd, HALF, axis))
    second = jnp.where(low, pltpu.roll(even, HALF, axis), odd)
    return first, second


def lane_of(values, index):
    tiles = values.reshape(-1, 8, NZ)
    tiles = [
        jnp.take_along_axis(tiles[n], index, axis=1, mode="promise_in_bounds") for n in range(tiles.shape[0])
    ]
    return jnp.stack(tiles).reshape(values.shape)


def beside(here, edge, repeat=False):
    whole = iota((8, NZ), 1)
    lane = whole % HALF
    sub = iota((8, NZ), 0)

    def bounded(mask, values):
        return values if edge is None else jnp.where(mask, edge, values)

    even, odd = here[:, 0:1], here[:, 1:2]
    same = jnp.concatenate([odd, even], axis=1)
    if repeat:
        left = lane_of(odd, jnp.where(lane == 0, whole, whole - 1))
        right = lane_of(even, jnp.where(lane == HALF - 1, whole, whole + 1))
    else:
        left = bounded(lane == 0, pltpu.roll(odd, 1, 4))
        right = bounded(lane == HALF - 1, pltpu.roll(even, NZ - 1, 4))
    rolled = jnp.concatenate([left, right], axis=1)
    down = bounded(sub == 0, pltpu.roll(here[:, :, 7:8], 1, 3))
    up = bounded(sub == 7, pltpu.roll(here[:, :, 0:1], 7, 3))
    below = jnp.concatenate([down, here[:, :, :7]], axis=2)
    above = jnp.concatenate([here[:, :, 1:], up], axis=2)
    return same, rolled, below, above


def sweeps(first, last, count, step, even, odd, block):
    for k in range(first, last + 1):
        before, after = (even, odd) if k % 2 == first % 2 else (odd, even)
        whole, rest = divmod(count - k, step)

        def body(j, carry, before=before, after=after, k=k):
            block(before, after, k + j * step, step)
            return carry

        lax.fori_loop(0, whole, body, 0)
        if rest:
            block(before, after, count - rest, rest)
        after[count] = pltpu.roll(after[count - 1], HALF, 3)
    return after


def prepare_kernel(meta, cells, out):
    core = meta[2]
    rows = [
        cells[pl.ds(layer * NY + 4 * core + i, 8, stride=8), :] for layer in range(4) for i in range(4)
    ]
    out[...] = moved(jnp.concatenate(rows), False)


def station_kernel(meta, sx, sy, sz, obs, count_out, seen_out, rhs):
    half, base = meta[0], meta[1]
    x, y, z = sx[...] - base, sy[...], sz[...]
    layer = jnp.minimum(x, ADJ - 1 - x)
    row = (layer * 2 + z % 2) * NY + (y % 8) * 8 + y // 8
    row = jnp.where(layer >= 0, row, -1)
    lane = jnp.where(x < ADJ // 2, 0, HALF) + z // 2
    seen = jnp.where(half == 0, obs[0:1, :], obs[1:2, :])
    there = iota((NZ, sx.shape[1]), 0) == lane
    for part, value in enumerate((jnp.ones_like(seen),) + parts(seen)):
        rhs[part * NZ : (part + 1) * NZ, :] = jnp.where(there, value, 0.0).astype(jnp.bfloat16)
    chunk = 256

    def body(step, carry):
        match = iota((chunk, sx.shape[1]), 0) + step * chunk == row
        match = jnp.where(match, 1.0, 0.0).astype(jnp.bfloat16)
        got = lax.dot_general(
            match, rhs[...], (((1,), (1,)), ((), ())), preferred_element_type=jnp.float32
        )
        where = pl.ds(pl.multiple_of(step * chunk, chunk), chunk)
        count_out[where, :] = got[:, :NZ]
        seen_out[where, :] = got[:, NZ : 2 * NZ] + got[:, 2 * NZ : 3 * NZ] + got[:, 3 * NZ :]
        return carry

    lax.fori_loop(0, ADJ * NY // chunk, body, 0)


def forward_kernel(meta, src_x, src_y, src_z, rows, lanes, mine, other, times_out, own_out, partner_out, slow, even, odd, table, picked, cells_in, times, arrived):
    half, core, offset, first = meta[0], meta[2], meta[3], meta[4]
    shape = (2, 8, 8, NZ)
    low = iota((8, NZ), 1) < HALF
    dy = iota(shape, 2) * 8 + iota(shape, 1) - src_y[half]
    dz = iota(shape, 3) % HALF * 2 + iota(shape, 0) - src_z[half]
    dist_yz = (dy * dy + dz * dz).astype(jnp.float32)
    row_x = jnp.where(low, first, first + WIDE - 1)
    sign = jnp.where(low, 1, -1)

    window = pl.ds(offset, WIDE)
    copies = [
        pltpu.make_async_copy(mine.at[window], cells_in.at[:, pl.ds(4 * core, 4)], arrived.at[0]),
        pltpu.make_async_copy(other.at[window], cells_in.at[:, pl.ds(4 - 4 * core, 4)], arrived.at[1]),
    ]
    for copy in copies:
        copy.start()
    for copy in copies:
        copy.wait()

    def load(layer, carry):
        cells = paired(cells_in[layer], cells_in[WIDE - 1 - layer], low)
        x = row_x + sign * layer
        inside = (x >= 0) & (x < NX)
        dx = (x - src_x[half]).astype(jnp.float32)
        start = START * SPACING * jnp.sqrt(dist_yz + dx * dx)
        slow[layer] = jnp.where(inside, SPACING * cells, BIG)
        even[layer] = jnp.where(inside, start + (0.5 * SPACING) * cells, BIG)
        return carry

    lax.fori_loop(0, WIDE // 2, load, 0, unroll=4)

    def block(before, after, layer, step):
        near = before[pl.ds(layer - 1, step + 2)]
        here = near[1 : step + 1]
        best = jnp.minimum(near[:step], near[2:])
        same, rolled, below, above = beside(here, BIG, True)
        best = jnp.minimum(best, jnp.minimum(same, rolled))
        best = jnp.minimum(best, jnp.minimum(below, above))
        after[pl.ds(layer, step)] = jnp.minimum(here, best + slow[pl.ds(layer, step)])

    even[WIDE // 2] = pltpu.roll(even[WIDE // 2 - 1], HALF, 3)
    last = sweeps(1, ITERS, WIDE // 2, 16, even, odd, block)

    def finish(j, carry):
        layer = ITERS + j
        x = row_x + sign * layer
        cells = last[layer] - 0.5 * slow[layer]
        cells = jnp.where((x >= 0) & (x < NX), cells, -BIG)
        table[pl.ds(pl.multiple_of(j * 2 * NY, 2 * NY), 2 * NY), :] = cells.reshape(2 * NY, NZ)
        times[j], times[SEEN - 1 - j] = parted(cells[0], cells[1], low)
        return carry

    lax.fori_loop(0, SEEN // 2, finish, 0, unroll=4)
    leaving = pltpu.make_async_copy(times, times_out, arrived.at[0])
    leaving.start()
    one = iota((1, NZ), 1)

    def pick(j, carry):
        line = table[pl.ds(rows[j], 1), :]
        picked[pl.ds(j, 1), :] = jnp.where(one == lanes[j], line, 0.0)
        return carry

    lax.fori_loop(0, picked.shape[0], pick, 0, unroll=16)
    arrive = lax.dot_general(
        jnp.ones((8, NZ), jnp.float32),
        picked[...],
        (((1,), (1,)), ((), ())),
        precision=lax.Precision.HIGHEST,
        preferred_element_type=jnp.float32,
    )
    own_out[...] = arrive[:, : arrive.shape[1] // 2]
    partner_out[...] = arrive[:, arrive.shape[1] // 2 :]
    leaving.wait()


def adjoint_kernel(meta, times_in, count_in, seen_in, out, coef, even, odd, natural, count, seen, times, arrived):
    entering = pltpu.make_async_copy(times_in.at[pl.ds(meta[5], ADJ)], times, arrived.at[2])
    entering.start()
    copies = [
        pltpu.make_async_copy(count_in, count, arrived.at[0]),
        pltpu.make_async_copy(seen_in, seen, arrived.at[1]),
    ]
    for copy in copies:
        copy.start()
    low = iota((8, NZ), 1) < HALF
    top = ADJ // 2

    entering.wait()

    def load(layer, carry):
        odd[layer] = paired(times[layer], times[ADJ - 1 - layer], low)
        return carry

    lax.fori_loop(0, top, load, 0, unroll=4)
    odd[top] = pltpu.roll(odd[top - 1], HALF, 3)
    for copy in copies:
        copy.wait()

    def weights(layer, size):
        where = pl.ds(layer, size)
        here = odd[where]
        others = (odd[pl.ds(layer + 1, size)], odd[pl.ds(layer - 1, size)]) + beside(here, -BIG)
        terms = [jnp.maximum(n - here, 0.0) * (1.0 / SPACING) for n in others]
        denom = 1.0 + terms[0] + terms[1] + terms[2] + terms[3] + terms[4] + terms[5]
        scale = 1.0 / denom
        for n, term in enumerate(terms):
            coef[n, where] = term * scale
        first = (count[where] * here - seen[where]) * scale
        coef[6, where] = first
        even[where] = first

    lax.fori_loop(0, (top - 1) // 4, lambda j, carry: (weights(1 + 4 * j, 4), carry)[1], 0)
    weights(top - 3, 3)
    even[top] = pltpu.roll(even[top - 1], HALF, 3)

    def block(before, after, layer, step):
        where = pl.ds(layer, step)
        near = before[pl.ds(layer - 1, step + 2)]
        same, rolled, below, above = beside(near[1 : step + 1], None)
        total = coef[6, where] + coef[0, where] * near[2:] + coef[1, where] * near[:step]
        total = total + coef[2, where] * same + coef[4, where] * below
        after[where] = total + (coef[3, where] * rolled + coef[5, where] * above)

    final = sweeps(2, ITERS, top, 8, even, odd, block)
    for j in range(LAYERS // 2):
        cells = final[ITERS + j]
        natural[j], natural[LAYERS - 1 - j] = parted(cells[0], cells[1], low)
    rows = moved(natural[...].reshape(LAYERS * NY, NZ), True)
    for layer in range(LAYERS):
        for i in range(8):
            at = (layer * 8 + i) * 8
            out[pl.ds(layer * 8 + i, 8, stride=64), :] = rows[at : at + 8]


def cycle(cells, axis, size, shift):
    return lax.ppermute(cells, axis, [(i, (i + shift) % size) for i in range(size)])


def gathered(part, y, half, beside_it):
    partner = cycle(part, "half", 2, 1)
    slab = jnp.where(
        half == 0, jnp.concatenate([part, partner]), jnp.concatenate([partner, part])
    )
    line = jnp.zeros((4,) + slab.shape, jnp.float32)
    line = lax.dynamic_update_index_in_dim(line, slab, y, 0)
    for shift in (1, 3, 2):
        line = lax.dynamic_update_index_in_dim(line, cycle(slab, "y", 4, shift), (y - shift) % 4, 0)
    block = line.reshape((32,) + slab.shape[1:])
    before = lax.ppermute(block, "x", [(0, 1), (1, 2), (2, 3)])
    after = lax.ppermute(block, "x", [(1, 0), (2, 1), (3, 2)])
    before, after, beside_it = lax.optimization_barrier((before, after, beside_it))
    mine = jnp.concatenate([before, block, after])
    return mine, cycle(mine, "core", 2, 1), beside_it


VMEM = pl.BlockSpec(memory_space=pltpu.VMEM)
ANY = pl.BlockSpec(memory_space=pl.ANY)
HBM = pl.BlockSpec(memory_space=pltpu.HBM)
SMEM = pl.BlockSpec(memory_space=pltpu.SMEM)


def f32(*shape):
    return jax.ShapeDtypeStruct(shape, jnp.float32)


def per_device(slowness, source_x, source_y, source_z, station_x, station_y, station_z, observed):
    core, x, y, half = (lax.axis_index(a) for a in ("core", "x", "y", "half"))
    group = lax.axis_index("zlo") * 2 + core
    slab = 4 * x + y
    back = jnp.where(y < 2, 16, 24)
    seen_first = slab * LAYERS - back
    slow_first = seen_first - ITERS
    meta = jnp.stack(
        [half, slab * LAYERS - ITERS, core, slow_first - 32 * (x - 1), slow_first, back - ITERS]
    ).astype(jnp.int32)

    stations = station_x.shape[0]

    def params(mib):
        return pltpu.CompilerParams(vmem_limit_bytes=mib * 1024 * 1024)

    def line_of(values):
        line = lax.dynamic_index_in_dim(values.reshape(4, 4, 2, stations // 32), y, 1, keepdims=False)
        own, partner = line[:, 0], line[:, 1]
        return jnp.where(half == 0, jnp.stack([own, partner]), jnp.stack([partner, own]))

    at_x, at_y, at_z = line_of(station_x), line_of(station_y), line_of(station_z)
    owned = at_x // 32 == x
    seen_x = at_x - seen_first
    layer = jnp.minimum(seen_x, SEEN - 1 - seen_x)
    row = (layer * 2 + at_z % 2) * NY + (at_y % 8) * 8 + at_y // 8
    rows = jnp.where(owned, row, 0).reshape(-1)
    lanes = jnp.where(owned, jnp.where(seen_x < SEEN // 2, 0, HALF) + at_z // 2, -1).reshape(-1)
    later, rows, lanes = lax.optimization_barrier((meta, rows, lanes))

    count, seen = pl.pallas_call(
        station_kernel,
        out_shape=(f32(ADJ * 64, NZ), f32(ADJ * 64, NZ)),
        in_specs=[SMEM, VMEM, VMEM, VMEM, VMEM],
        out_specs=(VMEM, VMEM),
        scratch_shapes=[pltpu.VMEM((4 * NZ, stations), jnp.bfloat16)],
        compiler_params=params(20),
        cost_estimate=pl.CostEstimate(
            flops=2 * ADJ * 64 * stations * 4 * NZ, bytes_accessed=2 * ADJ * 64 * NZ * 4, transcendentals=0
        ),
        name="stations",
    )(later, station_x.reshape(1, -1), station_y.reshape(1, -1), station_z.reshape(1, -1), observed)

    part = pl.pallas_call(
        prepare_kernel,
        out_shape=f32(128, NZ),
        in_specs=[SMEM, VMEM],
        out_specs=VMEM,
        compiler_params=params(8),
        name="prepare",
    )(meta, slowness.reshape(-1, NZ))
    mine, other, (count, seen) = gathered(part.reshape(4, 4, 8, NZ), y, half, (count, seen))
    times, own, partner = pl.pallas_call(
        forward_kernel,
        out_shape=(f32(SEEN, 8, 8, NZ), f32(8, stations // 8), f32(8, stations // 8)),
        in_specs=[SMEM] * 6 + [ANY, ANY],
        out_specs=(HBM, VMEM, VMEM),
        scratch_shapes=[
            pltpu.VMEM((WIDE // 2, 2, 8, 8, NZ), jnp.float32),
            pltpu.VMEM((WIDE // 2 + 1, 2, 8, 8, NZ), jnp.float32),
            pltpu.VMEM((WIDE // 2 + 1, 2, 8, 8, NZ), jnp.float32),
            pltpu.VMEM((SEEN * NY, NZ), jnp.float32),
            pltpu.VMEM((stations // 4, NZ), jnp.float32),
            pltpu.VMEM((WIDE, 8, 8, NZ), jnp.float32),
            pltpu.VMEM((SEEN, 8, 8, NZ), jnp.float32),
            pltpu.SemaphoreType.DMA((2,)),
        ],
        compiler_params=params(28),
        cost_estimate=pl.CostEstimate(
            flops=7 * ITERS * WIDE * 8192, bytes_accessed=WIDE * 8192 * 8, transcendentals=WIDE * 8192
        ),
        name="forward",
    )(meta, source_x, source_y, source_z, rows, lanes, mine, other)

    partner = cycle(partner, "half", 2, 1)

    pieces = pl.pallas_call(
        adjoint_kernel,
        out_shape=f32(512, NZ),
        in_specs=[SMEM, HBM, HBM, HBM],
        out_specs=VMEM,
        scratch_shapes=[
            pltpu.VMEM((7, ADJ // 2, 2, 8, 8, NZ), jnp.float32),
            pltpu.VMEM((ADJ // 2 + 1, 2, 8, 8, NZ), jnp.float32),
            pltpu.VMEM((ADJ // 2 + 1, 2, 8, 8, NZ), jnp.float32),
            pltpu.VMEM((LAYERS, 8, 8, NZ), jnp.float32),
            pltpu.VMEM((ADJ // 2, 2, 8, 8, NZ), jnp.float32),
            pltpu.VMEM((ADJ // 2, 2, 8, 8, NZ), jnp.float32),
            pltpu.VMEM((ADJ, 8, 8, NZ), jnp.float32),
            pltpu.SemaphoreType.DMA((3,)),
        ],
        compiler_params=params(56),
        cost_estimate=pl.CostEstimate(
            flops=12 * ITERS * ADJ * 8192, bytes_accessed=4 * ADJ * 8192 * 4, transcendentals=ADJ * 8192
        ),
        name="adjoint",
    )(
        meta,
        times,
        count.reshape(ADJ // 2, 2, 8, 8, NZ),
        seen.reshape(ADJ // 2, 2, 8, 8, NZ),
    )
    pieces, own, partner = lax.optimization_barrier((pieces, own, partner))
    summed = jnp.sum(
        lax.all_to_all(pieces.reshape(16, 4, 8, NZ), ("zlo", "core", "half"), 0, 0, tiled=True), axis=0
    )
    kernel = lax.dynamic_slice(slowness, (0, group * 8, 0), (4, 8, NZ)) * summed

    own, partner = own[0].reshape(4, stations // 32), partner[0].reshape(4, stations // 32)
    known = jnp.where(half == 0, jnp.stack([own, partner], 1), jnp.stack([partner, own], 1))
    arrivals = lax.dynamic_index_in_dim(known, x, 0, keepdims=False)
    for shift in (1, 2, 3):
        piece = lax.dynamic_index_in_dim(known, (x + shift) % 4, 0, keepdims=False)
        arrivals = arrivals + cycle(piece, "x", 4, shift)
    return kernel, arrivals


def solution(mesh):
    fine = Mesh(mesh.devices.reshape(4, 2, 4, 4, 2), ("zlo", "core", "x", "y", "half"))
    src, brick = ("zlo", "core"), ("x", "y", "half")
    in_specs = (P(brick, None, None), P(src), P(src), P(src), P(), P(), P(), P(src, None))
    out_specs = (P(brick, src, None), P(src, brick))
    return jax.shard_map(
        per_device, mesh=fine, in_specs=in_specs, out_specs=out_specs, check_vma=False
    )
```

```python
import jax
import jax.numpy as jnp
from jax import lax
from jax.experimental import pallas as pl
from jax.experimental.pallas import tpu as pltpu
from jax.sharding import Mesh, PartitionSpec as P

ITERS = 16
SPACING = 0.015625
BIG = 1000000.0
START = 2.0

LAYERS = 8
SEEN = 48
WIDE = SEEN + 2 * ITERS
ADJ = LAYERS + 2 * ITERS
NX, NY, NZ = 128, 64, 128
HALF = NZ // 2


def iota(shape, dim):
    return lax.broadcasted_iota(jnp.int32, shape, dim)


def parts(values):
    hi = values.astype(jnp.bfloat16).astype(jnp.float32)
    mid = (values - hi).astype(jnp.bfloat16).astype(jnp.float32)
    return hi, mid, values - hi - mid


def moved(values, inverse):
    z, lane = iota((NZ, NZ), 0), iota((NZ, NZ), 1)
    if inverse:
        z, lane = lane, z
    match = jnp.where((z % 2) * HALF + z // 2 == lane, 1.0, 0.0).astype(jnp.bfloat16)
    got = [
        jnp.dot(part.astype(jnp.bfloat16), match, preferred_element_type=jnp.float32)
        for part in parts(values)
    ]
    return got[0] + got[1] + got[2]


def paired(first, second, low):
    axis = first.ndim - 1
    even = jnp.where(low, first, pltpu.roll(second, HALF, axis))
    odd = jnp.where(low, pltpu.roll(first, HALF, axis), second)
    return jnp.stack([even, odd])


def parted(even, odd, low):
    axis = even.ndim - 1
    first = jnp.where(low, even, pltpu.roll(odd, HALF, axis))
    second = jnp.where(low, pltpu.roll(even, HALF, axis), odd)
    return first, second


def lane_of(values, index):
    tiles = values.reshape(-1, 8, NZ)
    tiles = [
        jnp.take_along_axis(tiles[n], index, axis=1, mode="promise_in_bounds") for n in range(tiles.shape[0])
    ]
    return jnp.stack(tiles).reshape(values.shape)


def beside(here, edge, repeat=False):
    whole = iota((8, NZ), 1)
    lane = whole % HALF
    sub = iota((8, NZ), 0)

    def bounded(mask, values):
        return values if edge is None else jnp.where(mask, edge, values)

    even, odd = here[:, 0:1], here[:, 1:2]
    same = jnp.concatenate([odd, even], axis=1)
    if repeat:
        left = lane_of(odd, jnp.where(lane == 0, whole, whole - 1))
        right = lane_of(even, jnp.where(lane == HALF - 1, whole, whole + 1))
    else:
        left = bounded(lane == 0, pltpu.roll(odd, 1, 4))
        right = bounded(lane == HALF - 1, pltpu.roll(even, NZ - 1, 4))
    rolled = jnp.concatenate([left, right], axis=1)
    down = bounded(sub == 0, pltpu.roll(here[:, :, 7:8], 1, 3))
    up = bounded(sub == 7, pltpu.roll(here[:, :, 0:1], 7, 3))
    below = jnp.concatenate([down, here[:, :, :7]], axis=2)
    above = jnp.concatenate([here[:, :, 1:], up], axis=2)
    return same, rolled, below, above


def sweeps(first, last, count, step, even, odd, block):
    for k in range(first, last + 1):
        before, after = (even, odd) if k % 2 == first % 2 else (odd, even)
        whole, rest = divmod(count - k, step)

        def body(j, carry, before=before, after=after, k=k):
            block(before, after, k + j * step, step)
            return carry

        lax.fori_loop(0, whole, body, 0)
        if rest:
            block(before, after, count - rest, rest)
        after[count] = pltpu.roll(after[count - 1], HALF, 3)
    return after


def prepare_kernel(meta, cells, out):
    core = meta[2]
    rows = [
        cells[pl.ds(layer * NY + 4 * core + i, 8, stride=8), :] for layer in range(4) for i in range(4)
    ]
    out[...] = moved(jnp.concatenate(rows), False)


def station_kernel(meta, sx, sy, sz, obs, count_out, seen_out, rhs):
    half, base = meta[0], meta[1]
    x, y, z = sx[...] - base, sy[...], sz[...]
    layer = jnp.minimum(x, ADJ - 1 - x)
    row = (layer * 2 + z % 2) * NY + (y % 8) * 8 + y // 8
    row = jnp.where(layer >= 0, row, -1)
    lane = jnp.where(x < ADJ // 2, 0, HALF) + z // 2
    seen = jnp.where(half == 0, obs[0:1, :], obs[1:2, :])
    there = iota((NZ, sx.shape[1]), 0) == lane
    for part, value in enumerate((jnp.ones_like(seen),) + parts(seen)):
        rhs[part * NZ : (part + 1) * NZ, :] = jnp.where(there, value, 0.0).astype(jnp.bfloat16)
    chunk = 256

    def body(step, carry):
        match = iota((chunk, sx.shape[1]), 0) + step * chunk == row
        match = jnp.where(match, 1.0, 0.0).astype(jnp.bfloat16)
        got = lax.dot_general(
            match, rhs[...], (((1,), (1,)), ((), ())), preferred_element_type=jnp.float32
        )
        where = pl.ds(pl.multiple_of(step * chunk, chunk), chunk)
        count_out[where, :] = got[:, :NZ]
        seen_out[where, :] = got[:, NZ : 2 * NZ] + got[:, 2 * NZ : 3 * NZ] + got[:, 3 * NZ :]
        return carry

    lax.fori_loop(0, ADJ * NY // chunk, body, 0)


def forward_kernel(meta, src_x, src_y, src_z, rows, lanes, mine, other, times_out, own_out, partner_out, slow, even, odd, table, picked):
    half, core, offset, first = meta[0], meta[2], meta[3], meta[4]
    shape = (2, 8, 8, NZ)
    low = iota((8, NZ), 1) < HALF
    dy = iota(shape, 2) * 8 + iota(shape, 1) - src_y[half]
    dz = iota(shape, 3) % HALF * 2 + iota(shape, 0) - src_z[half]
    dist_yz = (dy * dy + dz * dz).astype(jnp.float32)
    row_x = jnp.where(low, first, first + WIDE - 1)
    sign = jnp.where(low, 1, -1)

    def of_layer(layer):
        a, b = mine[offset + layer], other[offset + layer]
        return jnp.concatenate([jnp.where(core == 0, a, b), jnp.where(core == 0, b, a)], axis=0)

    def load(layer, carry):
        cells = paired(of_layer(layer), of_layer(WIDE - 1 - layer), low)
        x = row_x + sign * layer
        inside = (x >= 0) & (x < NX)
        dx = (x - src_x[half]).astype(jnp.float32)
        start = START * SPACING * jnp.sqrt(dist_yz + dx * dx)
        slow[layer] = jnp.where(inside, SPACING * cells, BIG)
        even[layer] = jnp.where(inside, start + (0.5 * SPACING) * cells, BIG)
        return carry

    lax.fori_loop(0, WIDE // 2, load, 0, unroll=4)

    def block(before, after, layer, step):
        near = before[pl.ds(layer - 1, step + 2)]
        here = near[1 : step + 1]
        best = jnp.minimum(near[:step], near[2:])
        same, rolled, below, above = beside(here, BIG, True)
        best = jnp.minimum(best, jnp.minimum(same, rolled))
        best = jnp.minimum(best, jnp.minimum(below, above))
        after[pl.ds(layer, step)] = jnp.minimum(here, best + slow[pl.ds(layer, step)])

    even[WIDE // 2] = pltpu.roll(even[WIDE // 2 - 1], HALF, 3)
    last = sweeps(1, ITERS, WIDE // 2, 16, even, odd, block)

    def finish(j, carry):
        layer = ITERS + j
        x = row_x + sign * layer
        cells = last[layer] - 0.5 * slow[layer]
        cells = jnp.where((x >= 0) & (x < NX), cells, -BIG)
        table[pl.ds(pl.multiple_of(j * 2 * NY, 2 * NY), 2 * NY), :] = cells.reshape(2 * NY, NZ)
        times_out[j], times_out[SEEN - 1 - j] = parted(cells[0], cells[1], low)
        return carry

    lax.fori_loop(0, SEEN // 2, finish, 0, unroll=4)
    one = iota((1, NZ), 1)

    def pick(j, carry):
        line = table[pl.ds(rows[j], 1), :]
        picked[pl.ds(j, 1), :] = jnp.where(one == lanes[j], line, 0.0)
        return carry

    lax.fori_loop(0, picked.shape[0], pick, 0, unroll=16)
    arrive = lax.dot_general(
        jnp.ones((8, NZ), jnp.float32),
        picked[...],
        (((1,), (1,)), ((), ())),
        precision=lax.Precision.HIGHEST,
        preferred_element_type=jnp.float32,
    )
    own_out[...] = arrive[:, : arrive.shape[1] // 2]
    partner_out[...] = arrive[:, arrive.shape[1] // 2 :]


def adjoint_kernel(meta, times, count, seen, out, coef, even, odd, natural):
    start = meta[5]
    low = iota((8, NZ), 1) < HALF
    top = ADJ // 2

    def load(layer, carry):
        odd[layer] = paired(times[start + layer], times[start + ADJ - 1 - layer], low)
        return carry

    lax.fori_loop(0, top, load, 0, unroll=4)
    odd[top] = pltpu.roll(odd[top - 1], HALF, 3)

    def weights(layer, size):
        where = pl.ds(layer, size)
        here = odd[where]
        others = (odd[pl.ds(layer + 1, size)], odd[pl.ds(layer - 1, size)]) + beside(here, -BIG)
        terms = [jnp.maximum(n - here, 0.0) * (1.0 / SPACING) for n in others]
        denom = 1.0 + terms[0] + terms[1] + terms[2] + terms[3] + terms[4] + terms[5]
        scale = 1.0 / denom
        for n, term in enumerate(terms):
            coef[n, where] = term * scale
        first = (count[where] * here - seen[where]) * scale
        coef[6, where] = first
        even[where] = first

    lax.fori_loop(0, (top - 1) // 4, lambda j, carry: (weights(1 + 4 * j, 4), carry)[1], 0)
    weights(top - 3, 3)
    even[top] = pltpu.roll(even[top - 1], HALF, 3)

    def block(before, after, layer, step):
        where = pl.ds(layer, step)
        near = before[pl.ds(layer - 1, step + 2)]
        same, rolled, below, above = beside(near[1 : step + 1], None)
        total = coef[6, where] + coef[0, where] * near[2:] + coef[1, where] * near[:step]
        total = total + coef[2, where] * same + coef[4, where] * below
        after[where] = total + (coef[3, where] * rolled + coef[5, where] * above)

    final = sweeps(2, ITERS, top, 8, even, odd, block)
    for j in range(LAYERS // 2):
        cells = final[ITERS + j]
        natural[j], natural[LAYERS - 1 - j] = parted(cells[0], cells[1], low)
    rows = moved(natural[...].reshape(LAYERS * NY, NZ), True)
    for layer in range(LAYERS):
        for i in range(8):
            at = (layer * 8 + i) * 8
            out[pl.ds(layer * 8 + i, 8, stride=64), :] = rows[at : at + 8]


def cycle(cells, axis, size, shift):
    return lax.ppermute(cells, axis, [(i, (i + shift) % size) for i in range(size)])


def gathered(part, y, half, beside_it):
    partner = cycle(part, "half", 2, 1)
    slab = jnp.where(
        half == 0, jnp.concatenate([part, partner]), jnp.concatenate([partner, part])
    )
    line = jnp.zeros((4,) + slab.shape, jnp.float32)
    line = lax.dynamic_update_index_in_dim(line, slab, y, 0)
    for shift in (1, 3, 2):
        line = lax.dynamic_update_index_in_dim(line, cycle(slab, "y", 4, shift), (y - shift) % 4, 0)
    block = line.reshape((32,) + slab.shape[1:])
    before = lax.ppermute(block, "x", [(0, 1), (1, 2), (2, 3)])
    after = lax.ppermute(block, "x", [(1, 0), (2, 1), (3, 2)])
    before, after, beside_it = lax.optimization_barrier((before, after, beside_it))
    mine = jnp.concatenate([before, block, after])
    return mine, cycle(mine, "core", 2, 1), beside_it


VMEM = pl.BlockSpec(memory_space=pltpu.VMEM)
SMEM = pl.BlockSpec(memory_space=pltpu.SMEM)


def f32(*shape):
    return jax.ShapeDtypeStruct(shape, jnp.float32)


def per_device(slowness, source_x, source_y, source_z, station_x, station_y, station_z, observed):
    core, x, y, half = (lax.axis_index(a) for a in ("core", "x", "y", "half"))
    group = lax.axis_index("zlo") * 2 + core
    slab = 4 * x + y
    back = jnp.where(y < 2, 16, 24)
    seen_first = slab * LAYERS - back
    slow_first = seen_first - ITERS
    meta = jnp.stack(
        [half, slab * LAYERS - ITERS, core, slow_first - 32 * (x - 1), slow_first, back - ITERS]
    ).astype(jnp.int32)

    stations = station_x.shape[0]

    def params(mib):
        return pltpu.CompilerParams(vmem_limit_bytes=mib * 1024 * 1024)

    def line_of(values):
        line = lax.dynamic_index_in_dim(values.reshape(4, 4, 2, stations // 32), y, 1, keepdims=False)
        own, partner = line[:, 0], line[:, 1]
        return jnp.where(half == 0, jnp.stack([own, partner]), jnp.stack([partner, own]))

    at_x, at_y, at_z = line_of(station_x), line_of(station_y), line_of(station_z)
    owned = at_x // 32 == x
    seen_x = at_x - seen_first
    layer = jnp.minimum(seen_x, SEEN - 1 - seen_x)
    row = (layer * 2 + at_z % 2) * NY + (at_y % 8) * 8 + at_y // 8
    rows = jnp.where(owned, row, 0).reshape(-1)
    lanes = jnp.where(owned, jnp.where(seen_x < SEEN // 2, 0, HALF) + at_z // 2, -1).reshape(-1)
    later, rows, lanes = lax.optimization_barrier((meta, rows, lanes))

    count, seen = pl.pallas_call(
        station_kernel,
        out_shape=(f32(ADJ * 64, NZ), f32(ADJ * 64, NZ)),
        in_specs=[SMEM, VMEM, VMEM, VMEM, VMEM],
        out_specs=(VMEM, VMEM),
        scratch_shapes=[pltpu.VMEM((4 * NZ, stations), jnp.bfloat16)],
        compiler_params=params(28),
        cost_estimate=pl.CostEstimate(
            flops=2 * ADJ * 64 * stations * 4 * NZ, bytes_accessed=2 * ADJ * 64 * NZ * 4, transcendentals=0
        ),
        name="stations",
    )(later, station_x.reshape(1, -1), station_y.reshape(1, -1), station_z.reshape(1, -1), observed)

    part = pl.pallas_call(
        prepare_kernel,
        out_shape=f32(128, NZ),
        in_specs=[SMEM, VMEM],
        out_specs=VMEM,
        compiler_params=params(28),
        name="prepare",
    )(meta, slowness.reshape(-1, NZ))
    mine, other, (count, seen) = gathered(part.reshape(4, 4, 8, NZ), y, half, (count, seen))
    times, own, partner = pl.pallas_call(
        forward_kernel,
        out_shape=(f32(SEEN, 8, 8, NZ), f32(8, stations // 8), f32(8, stations // 8)),
        in_specs=[SMEM] * 6 + [VMEM, VMEM],
        out_specs=(VMEM, VMEM, VMEM),
        scratch_shapes=[
            pltpu.VMEM((WIDE // 2, 2, 8, 8, NZ), jnp.float32),
            pltpu.VMEM((WIDE // 2 + 1, 2, 8, 8, NZ), jnp.float32),
            pltpu.VMEM((WIDE // 2 + 1, 2, 8, 8, NZ), jnp.float32),
            pltpu.VMEM((SEEN * NY, NZ), jnp.float32),
            pltpu.VMEM((stations // 4, NZ), jnp.float32),
        ],
        compiler_params=params(28),
        cost_estimate=pl.CostEstimate(
            flops=7 * ITERS * WIDE * 8192, bytes_accessed=WIDE * 8192 * 8, transcendentals=WIDE * 8192
        ),
        name="forward",
    )(meta, source_x, source_y, source_z, rows, lanes, mine, other)

    pieces = pl.pallas_call(
        adjoint_kernel,
        out_shape=f32(512, NZ),
        in_specs=[SMEM, VMEM, VMEM, VMEM],
        out_specs=VMEM,
        scratch_shapes=[
            pltpu.VMEM((7, ADJ // 2, 2, 8, 8, NZ), jnp.float32),
            pltpu.VMEM((ADJ // 2 + 1, 2, 8, 8, NZ), jnp.float32),
            pltpu.VMEM((ADJ // 2 + 1, 2, 8, 8, NZ), jnp.float32),
            pltpu.VMEM((LAYERS, 8, 8, NZ), jnp.float32),
        ],
        compiler_params=params(28),
        cost_estimate=pl.CostEstimate(
            flops=12 * ITERS * ADJ * 8192, bytes_accessed=4 * ADJ * 8192 * 4, transcendentals=ADJ * 8192
        ),
        name="adjoint",
    )(
        meta,
        times,
        count.reshape(ADJ // 2, 2, 8, 8, NZ),
        seen.reshape(ADJ // 2, 2, 8, 8, NZ),
    )
    pieces, own, partner = lax.optimization_barrier((pieces, own, partner))
    partner = cycle(partner, "half", 2, 1)
    summed = jnp.sum(
        lax.all_to_all(pieces.reshape(16, 4, 8, NZ), ("zlo", "core", "half"), 0, 0, tiled=True), axis=0
    )
    kernel = lax.dynamic_slice(slowness, (0, group * 8, 0), (4, 8, NZ)) * summed

    own, partner = own[0].reshape(4, stations // 32), partner[0].reshape(4, stations // 32)
    known = jnp.where(half == 0, jnp.stack([own, partner], 1), jnp.stack([partner, own], 1))
    arrivals = lax.dynamic_index_in_dim(known, x, 0, keepdims=False)
    for shift in (1, 2, 3):
        piece = lax.dynamic_index_in_dim(known, (x + shift) % 4, 0, keepdims=False)
        arrivals = arrivals + cycle(piece, "x", 4, shift)
    return kernel, arrivals


def solution(mesh):
    fine = Mesh(mesh.devices.reshape(4, 2, 4, 4, 2), ("zlo", "core", "x", "y", "half"))
    src, brick = ("zlo", "core"), ("x", "y", "half")
    in_specs = (P(brick, None, None), P(src), P(src), P(src), P(), P(), P(), P(src, None))
    out_specs = (P(brick, src, None), P(src, brick))
    return jax.shard_map(
        per_device, mesh=fine, in_specs=in_specs, out_specs=out_specs, check_vma=False
    )
```

```python
import jax
import jax.numpy as jnp
from jax import lax
from jax.experimental import pallas as pl
from jax.experimental.pallas import tpu as pltpu
from jax.sharding import Mesh, PartitionSpec as P

ITERS = 16
SPACING = 0.015625
BIG = 1000000.0
START = 2.0

LAYERS = 8
SEEN = 48
WIDE = SEEN + 2 * ITERS
ADJ = LAYERS + 2 * ITERS
NX, NY, NZ = 128, 64, 128
HALF = NZ // 2


def iota(shape, dim):
    return lax.broadcasted_iota(jnp.int32, shape, dim)


def parts(values):
    hi = values.astype(jnp.bfloat16).astype(jnp.float32)
    mid = (values - hi).astype(jnp.bfloat16).astype(jnp.float32)
    return hi, mid, values - hi - mid


def moved(values, inverse):
    z, lane = iota((NZ, NZ), 0), iota((NZ, NZ), 1)
    if inverse:
        z, lane = lane, z
    match = jnp.where((z % 2) * HALF + z // 2 == lane, 1.0, 0.0).astype(jnp.bfloat16)
    got = [
        jnp.dot(part.astype(jnp.bfloat16), match, preferred_element_type=jnp.float32)
        for part in parts(values)
    ]
    return got[0] + got[1] + got[2]


def paired(first, second, low):
    axis = first.ndim - 1
    even = jnp.where(low, first, pltpu.roll(second, HALF, axis))
    odd = jnp.where(low, pltpu.roll(first, HALF, axis), second)
    return jnp.stack([even, odd])


def parted(even, odd, low):
    axis = even.ndim - 1
    first = jnp.where(low, even, pltpu.roll(odd, HALF, axis))
    second = jnp.where(low, pltpu.roll(even, HALF, axis), odd)
    return first, second


def lane_of(values, index):
    tiles = values.reshape(-1, 8, NZ)
    tiles = [
        jnp.take_along_axis(tiles[n], index, axis=1, mode="promise_in_bounds") for n in range(tiles.shape[0])
    ]
    return jnp.stack(tiles).reshape(values.shape)


def beside(here, edge, repeat=False):
    whole = iota((8, NZ), 1)
    lane = whole % HALF
    sub = iota((8, NZ), 0)

    def bounded(mask, values):
        return values if edge is None else jnp.where(mask, edge, values)

    even, odd = here[:, 0:1], here[:, 1:2]
    same = jnp.concatenate([odd, even], axis=1)
    if repeat:
        left = lane_of(odd, jnp.where(lane == 0, whole, whole - 1))
        right = lane_of(even, jnp.where(lane == HALF - 1, whole, whole + 1))
    else:
        left = bounded(lane == 0, pltpu.roll(odd, 1, 4))
        right = bounded(lane == HALF - 1, pltpu.roll(even, NZ - 1, 4))
    rolled = jnp.concatenate([left, right], axis=1)
    down = bounded(sub == 0, pltpu.roll(here[:, :, 7:8], 1, 3))
    up = bounded(sub == 7, pltpu.roll(here[:, :, 0:1], 7, 3))
    below = jnp.concatenate([down, here[:, :, :7]], axis=2)
    above = jnp.concatenate([here[:, :, 1:], up], axis=2)
    return same, rolled, below, above


def sweeps(first, last, count, step, even, odd, block):
    for k in range(first, last + 1):
        before, after = (even, odd) if k % 2 == first % 2 else (odd, even)
        whole, rest = divmod(count - k, step)

        def body(j, carry, before=before, after=after, k=k):
            block(before, after, k + j * step, step)
            return carry

        lax.fori_loop(0, whole, body, 0)
        if rest:
            block(before, after, count - rest, rest)
        after[count] = pltpu.roll(after[count - 1], HALF, 3)
    return after


def prepare_kernel(meta, cells, out):
    core = meta[2]
    rows = [
        cells[pl.ds(layer * NY + 4 * core + i, 8, stride=8), :] for layer in range(4) for i in range(4)
    ]
    out[...] = moved(jnp.concatenate(rows), False)


def station_kernel(meta, sx, sy, sz, obs, count_out, seen_out, rhs):
    half, base = meta[0], meta[1]
    x, y, z = sx[...] - base, sy[...], sz[...]
    layer = jnp.minimum(x, ADJ - 1 - x)
    row = (layer * 2 + z % 2) * NY + (y % 8) * 8 + y // 8
    row = jnp.where(layer >= 0, row, -1)
    lane = jnp.where(x < ADJ // 2, 0, HALF) + z // 2
    seen = jnp.where(half == 0, obs[0:1, :], obs[1:2, :])
    there = iota((NZ, sx.shape[1]), 0) == lane
    for part, value in enumerate((jnp.ones_like(seen),) + parts(seen)):
        rhs[part * NZ : (part + 1) * NZ, :] = jnp.where(there, value, 0.0).astype(jnp.bfloat16)
    chunk = 256

    def body(step, carry):
        match = iota((chunk, sx.shape[1]), 0) + step * chunk == row
        match = jnp.where(match, 1.0, 0.0).astype(jnp.bfloat16)
        got = lax.dot_general(
            match, rhs[...], (((1,), (1,)), ((), ())), preferred_element_type=jnp.float32
        )
        where = pl.ds(pl.multiple_of(step * chunk, chunk), chunk)
        count_out[where, :] = got[:, :NZ]
        seen_out[where, :] = got[:, NZ : 2 * NZ] + got[:, 2 * NZ : 3 * NZ] + got[:, 3 * NZ :]
        return carry

    lax.fori_loop(0, ADJ * NY // chunk, body, 0)


def forward_kernel(meta, src_x, src_y, src_z, rows, lanes, mine, other, times_out, own_out, partner_out, slow, even, odd, table, picked):
    half, core, offset, first = meta[0], meta[2], meta[3], meta[4]
    shape = (2, 8, 8, NZ)
    low = iota((8, NZ), 1) < HALF
    dy = iota(shape, 2) * 8 + iota(shape, 1) - src_y[half]
    dz = iota(shape, 3) % HALF * 2 + iota(shape, 0) - src_z[half]
    dist_yz = (dy * dy + dz * dz).astype(jnp.float32)
    row_x = jnp.where(low, first, first + WIDE - 1)
    sign = jnp.where(low, 1, -1)

    def of_layer(layer):
        a, b = mine[offset + layer], other[offset + layer]
        return jnp.concatenate([jnp.where(core == 0, a, b), jnp.where(core == 0, b, a)], axis=0)

    def load(layer, carry):
        cells = paired(of_layer(layer), of_layer(WIDE - 1 - layer), low)
        x = row_x + sign * layer
        inside = (x >= 0) & (x < NX)
        dx = (x - src_x[half]).astype(jnp.float32)
        start = START * SPACING * jnp.sqrt(dist_yz + dx * dx)
        slow[layer] = jnp.where(inside, SPACING * cells, BIG)
        even[layer] = jnp.where(inside, start + (0.5 * SPACING) * cells, BIG)
        return carry

    lax.fori_loop(0, WIDE // 2, load, 0, unroll=4)

    def block(before, after, layer, step):
        near = before[pl.ds(layer - 1, step + 2)]
        here = near[1 : step + 1]
        best = jnp.minimum(near[:step], near[2:])
        same, rolled, below, above = beside(here, BIG, True)
        best = jnp.minimum(best, jnp.minimum(same, rolled))
        best = jnp.minimum(best, jnp.minimum(below, above))
        after[pl.ds(layer, step)] = jnp.minimum(here, best + slow[pl.ds(layer, step)])

    even[WIDE // 2] = pltpu.roll(even[WIDE // 2 - 1], HALF, 3)
    last = sweeps(1, ITERS, WIDE // 2, 16, even, odd, block)

    def finish(j, carry):
        layer = ITERS + j
        x = row_x + sign * layer
        cells = last[layer] - 0.5 * slow[layer]
        cells = jnp.where((x >= 0) & (x < NX), cells, -BIG)
        table[pl.ds(pl.multiple_of(j * 2 * NY, 2 * NY), 2 * NY), :] = cells.reshape(2 * NY, NZ)
        times_out[j], times_out[SEEN - 1 - j] = parted(cells[0], cells[1], low)
        return carry

    lax.fori_loop(0, SEEN // 2, finish, 0, unroll=4)
    one = iota((1, NZ), 1)

    def pick(j, carry):
        line = table[pl.ds(rows[j], 1), :]
        picked[pl.ds(j, 1), :] = jnp.where(one == lanes[j], line, 0.0)
        return carry

    lax.fori_loop(0, picked.shape[0], pick, 0, unroll=16)
    arrive = lax.dot_general(
        jnp.ones((8, NZ), jnp.float32),
        picked[...],
        (((1,), (1,)), ((), ())),
        precision=lax.Precision.HIGHEST,
        preferred_element_type=jnp.float32,
    )
    own_out[...] = arrive[:, : arrive.shape[1] // 2]
    partner_out[...] = arrive[:, arrive.shape[1] // 2 :]


def adjoint_kernel(meta, times, count, seen, out, coef, even, odd, natural):
    start = meta[5]
    low = iota((8, NZ), 1) < HALF
    top = ADJ // 2

    def load(layer, carry):
        odd[layer] = paired(times[start + layer], times[start + ADJ - 1 - layer], low)
        return carry

    lax.fori_loop(0, top, load, 0, unroll=4)
    odd[top] = pltpu.roll(odd[top - 1], HALF, 3)

    def weights(layer, size):
        where = pl.ds(layer, size)
        here = odd[where]
        others = (odd[pl.ds(layer + 1, size)], odd[pl.ds(layer - 1, size)]) + beside(here, -BIG)
        terms = [jnp.maximum(n - here, 0.0) * (1.0 / SPACING) for n in others]
        denom = 1.0 + terms[0] + terms[1] + terms[2] + terms[3] + terms[4] + terms[5]
        scale = 1.0 / denom
        for n, term in enumerate(terms):
            coef[n, where] = term * scale
        first = (count[where] * here - seen[where]) * scale
        coef[6, where] = first
        even[where] = first

    lax.fori_loop(0, (top - 1) // 4, lambda j, carry: (weights(1 + 4 * j, 4), carry)[1], 0)
    weights(top - 3, 3)
    even[top] = pltpu.roll(even[top - 1], HALF, 3)

    def block(before, after, layer, step):
        where = pl.ds(layer, step)
        near = before[pl.ds(layer - 1, step + 2)]
        same, rolled, below, above = beside(near[1 : step + 1], None)
        total = coef[6, where] + coef[0, where] * near[2:] + coef[1, where] * near[:step]
        total = total + coef[2, where] * same + coef[4, where] * below
        after[where] = total + (coef[3, where] * rolled + coef[5, where] * above)

    final = sweeps(2, ITERS, top, 8, even, odd, block)
    for j in range(LAYERS // 2):
        cells = final[ITERS + j]
        natural[j], natural[LAYERS - 1 - j] = parted(cells[0], cells[1], low)
    rows = moved(natural[...].reshape(LAYERS * NY, NZ), True)
    for layer in range(LAYERS):
        for i in range(8):
            at = (layer * 8 + i) * 8
            out[pl.ds(layer * 8 + i, 8, stride=64), :] = rows[at : at + 8]


def cycle(cells, axis, size, shift):
    return lax.ppermute(cells, axis, [(i, (i + shift) % size) for i in range(size)])


def gathered(part, y, half, beside_it):
    partner = cycle(part, "half", 2, 1)
    slab = jnp.where(
        half == 0, jnp.concatenate([part, partner]), jnp.concatenate([partner, part])
    )
    line = jnp.zeros((4,) + slab.shape, jnp.float32)
    line = lax.dynamic_update_index_in_dim(line, slab, y, 0)
    for shift in (1, 3, 2):
        line = lax.dynamic_update_index_in_dim(line, cycle(slab, "y", 4, shift), (y - shift) % 4, 0)
    block = line.reshape((32,) + slab.shape[1:])
    before = lax.ppermute(block, "x", [(0, 1), (1, 2), (2, 3)])
    after = lax.ppermute(block, "x", [(1, 0), (2, 1), (3, 2)])
    before, after, beside_it = lax.optimization_barrier((before, after, beside_it))
    mine = jnp.concatenate([before, block, after])
    return mine, cycle(mine, "core", 2, 1), beside_it


VMEM = pl.BlockSpec(memory_space=pltpu.VMEM)
SMEM = pl.BlockSpec(memory_space=pltpu.SMEM)


def f32(*shape):
    return jax.ShapeDtypeStruct(shape, jnp.float32)


def per_device(slowness, source_x, source_y, source_z, station_x, station_y, station_z, observed):
    core, x, y, half = (lax.axis_index(a) for a in ("core", "x", "y", "half"))
    group = lax.axis_index("zlo") * 2 + core
    slab = 4 * x + y
    back = jnp.where(y < 2, 16, 24)
    seen_first = slab * LAYERS - back
    slow_first = seen_first - ITERS
    meta = jnp.stack(
        [half, slab * LAYERS - ITERS, core, slow_first - 32 * (x - 1), slow_first, back - ITERS]
    ).astype(jnp.int32)

    stations = station_x.shape[0]

    def params(mib):
        return pltpu.CompilerParams(vmem_limit_bytes=mib * 1024 * 1024)

    def line_of(values):
        line = lax.dynamic_index_in_dim(values.reshape(4, 4, 2, stations // 32), y, 1, keepdims=False)
        own, partner = line[:, 0], line[:, 1]
        return jnp.where(half == 0, jnp.stack([own, partner]), jnp.stack([partner, own]))

    at_x, at_y, at_z = line_of(station_x), line_of(station_y), line_of(station_z)
    owned = at_x // 32 == x
    seen_x = at_x - seen_first
    layer = jnp.minimum(seen_x, SEEN - 1 - seen_x)
    row = (layer * 2 + at_z % 2) * NY + (at_y % 8) * 8 + at_y // 8
    rows = jnp.where(owned, row, 0).reshape(-1)
    lanes = jnp.where(owned, jnp.where(seen_x < SEEN // 2, 0, HALF) + at_z // 2, -1).reshape(-1)
    later, rows, lanes = lax.optimization_barrier((meta, rows, lanes))

    count, seen = pl.pallas_call(
        station_kernel,
        out_shape=(f32(ADJ * 64, NZ), f32(ADJ * 64, NZ)),
        in_specs=[SMEM, VMEM, VMEM, VMEM, VMEM],
        out_specs=(VMEM, VMEM),
        scratch_shapes=[pltpu.VMEM((4 * NZ, stations), jnp.bfloat16)],
        compiler_params=params(28),
        cost_estimate=pl.CostEstimate(
            flops=2 * ADJ * 64 * stations * 4 * NZ, bytes_accessed=2 * ADJ * 64 * NZ * 4, transcendentals=0
        ),
        name="stations",
    )(later, station_x.reshape(1, -1), station_y.reshape(1, -1), station_z.reshape(1, -1), observed)

    part = pl.pallas_call(
        prepare_kernel,
        out_shape=f32(128, NZ),
        in_specs=[SMEM, VMEM],
        out_specs=VMEM,
        compiler_params=params(28),
        name="prepare",
    )(meta, slowness.reshape(-1, NZ))
    piece_slow = lax.dynamic_slice(slowness, (0, group * 8, 0), (4, 8, NZ))
    mine, other, (count, seen, piece_slow) = gathered(
        part.reshape(4, 4, 8, NZ), y, half, (count, seen, piece_slow)
    )
    times, own, partner = pl.pallas_call(
        forward_kernel,
        out_shape=(f32(SEEN, 8, 8, NZ), f32(8, stations // 8), f32(8, stations // 8)),
        in_specs=[SMEM] * 6 + [VMEM, VMEM],
        out_specs=(VMEM, VMEM, VMEM),
        scratch_shapes=[
            pltpu.VMEM((WIDE // 2, 2, 8, 8, NZ), jnp.float32),
            pltpu.VMEM((WIDE // 2 + 1, 2, 8, 8, NZ), jnp.float32),
            pltpu.VMEM((WIDE // 2 + 1, 2, 8, 8, NZ), jnp.float32),
            pltpu.VMEM((SEEN * NY, NZ), jnp.float32),
            pltpu.VMEM((stations // 4, NZ), jnp.float32),
        ],
        compiler_params=params(28),
        cost_estimate=pl.CostEstimate(
            flops=7 * ITERS * WIDE * 8192, bytes_accessed=WIDE * 8192 * 8, transcendentals=WIDE * 8192
        ),
        name="forward",
    )(meta, source_x, source_y, source_z, rows, lanes, mine, other)

    pieces = pl.pallas_call(
        adjoint_kernel,
        out_shape=f32(512, NZ),
        in_specs=[SMEM, VMEM, VMEM, VMEM],
        out_specs=VMEM,
        scratch_shapes=[
            pltpu.VMEM((7, ADJ // 2, 2, 8, 8, NZ), jnp.float32),
            pltpu.VMEM((ADJ // 2 + 1, 2, 8, 8, NZ), jnp.float32),
            pltpu.VMEM((ADJ // 2 + 1, 2, 8, 8, NZ), jnp.float32),
            pltpu.VMEM((LAYERS, 8, 8, NZ), jnp.float32),
        ],
        compiler_params=params(28),
        cost_estimate=pl.CostEstimate(
            flops=12 * ITERS * ADJ * 8192, bytes_accessed=4 * ADJ * 8192 * 4, transcendentals=ADJ * 8192
        ),
        name="adjoint",
    )(
        meta,
        times,
        count.reshape(ADJ // 2, 2, 8, 8, NZ),
        seen.reshape(ADJ // 2, 2, 8, 8, NZ),
    )
    pieces, own, partner = lax.optimization_barrier((pieces, own, partner))
    partner = cycle(partner, "half", 2, 1)
    summed = jnp.sum(
        lax.all_to_all(pieces.reshape(16, 4, 8, NZ), ("zlo", "core", "half"), 0, 0, tiled=True), axis=0
    )
    kernel = piece_slow * summed

    own, partner = own[0].reshape(4, stations // 32), partner[0].reshape(4, stations // 32)
    known = jnp.where(half == 0, jnp.stack([own, partner], 1), jnp.stack([partner, own], 1))
    arrivals = lax.dynamic_index_in_dim(known, x, 0, keepdims=False)
    for shift in (1, 2, 3):
        piece = lax.dynamic_index_in_dim(known, (x + shift) % 4, 0, keepdims=False)
        arrivals = arrivals + cycle(piece, "x", 4, shift)
    return kernel, arrivals


def solution(mesh):
    fine = Mesh(mesh.devices.reshape(4, 2, 4, 4, 2), ("zlo", "core", "x", "y", "half"))
    src, brick = ("zlo", "core"), ("x", "y", "half")
    in_specs = (P(brick, None, None), P(src), P(src), P(src), P(), P(), P(), P(src, None))
    out_specs = (P(brick, src, None), P(src, brick))
    return jax.shard_map(
        per_device, mesh=fine, in_specs=in_specs, out_specs=out_specs, check_vma=False
    )
```
